512 devices in a mesh: idx: 64 (over x, z), rep: 8 (over y, core).
Axes of the slice: x: 4, y: 4, z: 16, core: 2. Of those that a mesh axis runs over, the one named last changes fastest.
Arguments:
- t_slab: bfloat16 [12800, 51200], P(('idx', 'rep')), may hold values from -6 to 6
- w_cycle: bfloat16 [51200, 400], P(('idx', 'rep')), may hold values from -0.078125 to 0.078125
- a_irrep: int32 [128], replicated, may hold values from 0 to 7
- b_irrep: int32 [4], replicated, may hold values from 0 to 7
- c_irrep: int32 [512], replicated, may hold values from 0 to 7, as said below
- occ_irrep: int32 [100], replicated, may hold values from 0 to 7
- eps_a: float32 [128], replicated, may hold values from 0.5 to 4
- eps_b: float32 [4], replicated, may hold values from 0.5 to 4
- eps_occ: float32 [100], replicated, may hold values from -3 to -0.5
Outputs:
- update: float32 [12800, 400], P(('idx', 'rep'))
The draws below stay inside these ranges and needn't reach their ends.
Inputs may be any that keep to these rules, and one draw needn't show every extreme that they name: `a_irrep`: D2h irrep labels; the product of two irreps is the bitwise exclusive or of their labels. `b_irrep`: D2h irrep labels. `c_irrep`: D2h irrep labels; each aligned group of 8 consecutive summed virtual orbitals holds each of the 8 irreps exactly once. `occ_irrep`: D2h irrep labels.
All inputs are finite; a program needn't handle non-finite values.
Results may differ from the reference program's by a relative error of at most 0.0003.
Values may be sent and summed in bfloat16 or wider, within the bound.
No kernel may reach another device: no remote copies, remote signals or barrier semaphores. Data moves between devices by JAX's collectives and lax.ppermute only.
A program may use at most 64 MiB of HBM per device.

```python
import jax
import jax.numpy as jnp
from jax import lax

O = 100
CV = 512
B = 4
A = 128


def draw_c_irrep(key, part):
    key = jax.random.fold_in(key, 11)
    groups = jax.random.split(key, CV // 8)
    labels = jax.vmap(lambda single: jax.random.permutation(single, 8))(groups)
    return labels.reshape(-1).astype(jnp.int32)


def place_ends(drawn, key, smallest, top_value):
    dims = drawn.shape
    spot = [jax.random.randint(jax.random.fold_in(key, axis), (), 0, dims[axis]) for axis in range(len(dims))]
    drawn = drawn.at[tuple(spot)].set(smallest)
    longest = dims.index(max(dims))
    spot[longest] = (spot[longest] + 1) % dims[longest]
    return drawn.at[tuple(spot)].set(top_value)


def shard_levels(key, extent, cuts, least, high):
    factor_of = 1.0
    for axis_at, shards_of in cuts:
        steps = jax.random.uniform(jax.random.fold_in(jax.random.fold_in(key, 6), axis_at), (shards_of,), jnp.float32, least / len(cuts), high / len(cuts))
        factor_of = factor_of * jnp.repeat(jnp.exp(steps), extent[axis_at] // shards_of).reshape((-1,) + (1,) * (len(extent) - 1 - axis_at))
    return factor_of


def normal_values(rng, extent, scale, reach, cuts=(), kind=jnp.bfloat16):
    gain = shard_levels(rng, extent, cuts, -0.22, 0.18) if cuts else 1.0
    drawn = jax.random.normal(rng, extent, jnp.float32) * scale * gain
    return jnp.minimum(jnp.maximum(drawn, -reach), reach).astype(kind)


def setup_inputs(seed: int = 0) -> dict:
    key_of = jax.random.split(jax.random.key(seed), 10)
    t_slab = normal_values(key_of[0], (A * O, CV * O), 1.0, 6.0, ((0, 512),))
    w_cycle = normal_values(key_of[1], (CV * O, B * O), (CV * O // 8) ** -0.5, 0.078125, ((0, 512),))
    a_irrep = place_ends(jax.random.randint(key_of[2], (A,), 0, 8), jax.random.fold_in(key_of[2], 1), 0, 7).astype(jnp.int32)
    b_irrep = place_ends(jax.random.randint(key_of[3], (B,), 0, 8), jax.random.fold_in(key_of[3], 1), 0, 7).astype(jnp.int32)
    c_irrep = draw_c_irrep(jax.random.fold_in(key_of[9], 71), 0)
    occ_irrep = place_ends(jax.random.randint(key_of[5], (O,), 0, 8), jax.random.fold_in(key_of[5], 1), 0, 7).astype(jnp.int32)
    eps_a = jnp.clip(jax.random.uniform(key_of[6], (A,), jnp.float32, 0.5, 4.0), 0.5, 4.0)
    eps_b = jnp.clip(jax.random.uniform(key_of[7], (B,), jnp.float32, 0.5, 4.0), 0.5, 4.0)
    eps_occ = jnp.clip(jax.random.uniform(key_of[8], (O,), jnp.float32, -3.0, -0.5), -3.0, -0.5)
    return dict(t_slab=t_slab, w_cycle=w_cycle, a_irrep=a_irrep, b_irrep=b_irrep, c_irrep=c_irrep, occ_irrep=occ_irrep, eps_a=eps_a, eps_b=eps_b, eps_occ=eps_occ)


def reference(t_slab, w_cycle, a_irrep, b_irrep, c_irrep, occ_irrep, eps_a, eps_b, eps_occ):
    row_label = jnp.bitwise_xor(a_irrep[:, None], occ_irrep[None, :])
    col_label = jnp.bitwise_xor(c_irrep[:, None], occ_irrep[None, :]).reshape(-1)
    out_label = jnp.bitwise_xor(b_irrep[:, None], occ_irrep[None, :]).reshape(-1)
    w_sym = jnp.where(col_label[:, None] == out_label[None, :], w_cycle, jnp.zeros((), w_cycle.dtype)).astype(jnp.float32)
    out_energy = (eps_b[:, None] - eps_occ[None, :]).reshape(-1)
    row_energy = eps_a[:, None] - eps_occ[None, :]
    slabs = t_slab.reshape(A, O, CV * O)

    def one_slab(pieces):
        rows, labels, energy = pieces
        masked = jnp.where(labels[:, None] == col_label[None, :], rows, jnp.zeros((), rows.dtype)).astype(jnp.float32)
        cycle = jnp.dot(masked, w_sym, precision=lax.Precision.HIGHEST)
        return cycle / (energy[:, None] + out_energy[None, :])

    result = lax.map(one_slab, (slabs, row_label, row_energy))
    return result.reshape(A * O, B * O)
```

```python
import jax
import jax.numpy as jnp
import numpy as np
from jax import lax
from jax.experimental import pallas as pl
from jax.experimental.pallas import tpu as pltpu
from jax.sharding import PartitionSpec as P

O = 100
G = 8
KP = 32
NP = 256
RP = 32
ROWS = 25
CHUNK = 4 * G * O
F32, BF16, I32 = jnp.float32, jnp.bfloat16, jnp.int32
VMEM = pl.BlockSpec(memory_space=pltpu.VMEM)
SMEM = pl.BlockSpec(memory_space=pltpu.SMEM)
ZS, XS, YS, CS = 16, 4, 4, 2
Z_GROUPS = [[x * ZS + z for z in range(ZS)] for x in range(XS)]
X_GROUPS = [[x * ZS + z for x in range(XS)] for z in range(ZS)]


def iota(shape, dim):
    return lax.broadcasted_iota(I32, shape, dim)


def to_rows(lanes, count, first):
    shape = (count, lanes.shape[1])
    hit = iota(shape, 1) == iota(shape, 0) + first
    return jnp.sum(jnp.where(hit, lanes, 0.0), axis=1, keepdims=True)


def tiled(lanes, width):
    rows = to_rows(lanes, 104, 0)
    shape = (104, width)
    s = iota(shape, 1)
    mod = s - O * ((s >= O).astype(I32) + (s >= 2 * O).astype(I32) + (s >= 3 * O).astype(I32))
    return jnp.sum(jnp.where(iota(shape, 0) == mod, rows, 0.0), axis=0, keepdims=True)


def by_slab(ref, width, dtype):
    s = iota((1, width), 1)
    out = jnp.full((1, width), ref[0], dtype)
    for b in range(1, 4):
        out = jnp.where(s >= b * O, ref[b], out)
    return out


def w_kernel(place, c_irrep, b_irrep, occ, w_ref, out_ref):
    occ_f = occ[...].astype(F32)
    row = c_irrep[place[0]] ^ to_rows(occ_f, 100, 0).astype(I32)
    col = by_slab(b_irrep, 400, I32) ^ tiled(occ_f, 400).astype(I32)
    kept = jnp.where(row == col, w_ref[...].astype(F32), 0.0)
    full = jnp.concatenate([kept, jnp.zeros((28, 400), F32)], axis=0)
    for y in range(YS):
        part = full[KP * y : KP * y + KP].astype(BF16)
        out_ref[CS * y] = part[:, :NP]
        out_ref[CS * y + 1, :, : 400 - NP] = part[:, NP:]
        out_ref[CS * y + 1, :, 400 - NP :] = jnp.zeros((KP, 2 * NP - 400), BF16)


def t_kernel(place, a_irrep, occ, c_rows, spread, tile, pick, t_ref, out_ref, want, have, kept):
    step = pl.program_id(0)

    @pl.when(step == 0)
    def _():
        occ_f = occ[...].astype(F32)
        row = a_irrep[place[0] // 4] ^ to_rows(occ_f, RP, ROWS * (place[0] % 4)).astype(I32)
        occ_t = jnp.dot(
            jnp.broadcast_to(occ_f, (8, O)).astype(BF16), tile[...], preferred_element_type=F32
        )
        want[...] = (row ^ occ_t[:1].astype(I32)).astype(BF16)
        have[...] = jnp.dot(
            c_rows[...].astype(F32).astype(BF16), spread[...], preferred_element_type=F32
        )
        kept[...] = jnp.zeros_like(kept)

    for h in range(2):
        label = have[pl.ds(2 * step + h, 1), :].astype(BF16)
        mask = want[:ROWS, :] == label
        block = t_ref[:, CHUNK * h : CHUNK * (h + 1)]
        kept[RP * h : RP * h + ROWS, :] = jnp.where(mask, block, jnp.zeros((), BF16))
    packed = jnp.dot(kept[...], pick[...], preferred_element_type=F32).astype(BF16)
    for h in range(2):
        for y in range(YS):
            part = packed[RP * h : RP * h + RP, 128 * y : 128 * y + 128]
            for c in range(CS):
                out_ref[CS * y + c, :, pl.ds(pl.multiple_of(256 * step + 128 * h, 128), 128)] = part


def mm_kernel(t_ref, w_ref, out_ref):
    out_ref[...] = jnp.dot(t_ref[...], w_ref[...], preferred_element_type=F32)


def end_kernel(place, a_irrep, b_irrep, eps_a, eps_b, occ, eps_occ, part_ref, out_ref):
    first = ROWS * (place[0] % 4)
    a = place[0] // 4
    occ_f = occ[...].astype(F32)
    eo = eps_occ[...]
    row = a_irrep[a] ^ to_rows(occ_f, ROWS, first).astype(I32)
    col = by_slab(b_irrep, 400, I32) ^ tiled(occ_f, 400).astype(I32)
    energy = (eps_a[a] - to_rows(eo, ROWS, first)) + (by_slab(eps_b, 400, F32) - tiled(eo, 400))
    for c, lo, hi in ((0, 0, NP), (1, NP, 400)):
        total = part_ref[c, :ROWS, : hi - lo]
        for y in range(1, YS):
            total = total + part_ref[CS * y + c, :ROWS, : hi - lo]
        total = jnp.where(row == col[:, lo:hi], total, 0.0)
        out_ref[:, lo:hi] = total / energy[:, lo:hi]


def tables():
    lane = np.arange(CHUNK)
    j, k = lane // (G * O), lane % O
    spread = (np.arange(32)[:, None] == lane[None, :] // O).astype(jnp.bfloat16)
    tile = (np.arange(O)[:, None] == k[None, :]).astype(jnp.bfloat16)
    target = (k // KP) * 128 + j * KP + k % KP
    pick = (target[:, None] == np.arange(512)[None, :]).astype(jnp.bfloat16)
    return spread, tile, pick


def call(kernel, shape, dtype, specs, flops, moved, **rest):
    return pl.pallas_call(
        kernel,
        out_shape=jax.ShapeDtypeStruct(shape, dtype),
        in_specs=specs,
        cost_estimate=pl.CostEstimate(flops=flops, bytes_accessed=moved, transcendentals=0),
        compiler_params=pltpu.CompilerParams(vmem_limit_bytes=40 * 2**20),
        **rest,
    )


def per_device(t_slab, w_cycle, a_irrep, b_irrep, c_irrep, occ_irrep, eps_a, eps_b, eps_occ):
    place = (lax.axis_index("idx") * (YS * CS) + lax.axis_index("rep")).astype(I32).reshape(1)
    occ = occ_irrep.reshape(1, O)
    spread, tile, pick = (jnp.asarray(table) for table in tables())
    w_parts = call(
        w_kernel, (8, KP, NP), BF16, [SMEM, SMEM, SMEM, VMEM, VMEM], 10**6, 2 * 10**5,
        out_specs=VMEM,
    )(place, c_irrep, b_irrep, occ, w_cycle)
    w_got = lax.all_to_all(w_parts, "rep", split_axis=0, concat_axis=0, tiled=True)
    w_own = jnp.sum(w_got, axis=0, dtype=BF16)

    const = lambda *shape: pl.BlockSpec(shape, lambda i: (0,) * len(shape))
    t_parts = call(
        t_kernel, (8, RP, 64 * KP), BF16,
        [SMEM, SMEM, const(1, O), const(16, 32), const(32, CHUNK), const(O, CHUNK), const(CHUNK, 512),
         pl.BlockSpec((ROWS, 2 * CHUNK), lambda i: (0, i))],
        2 * 512 * CHUNK * 512, 8 * 10**6,
        grid=(8,),
        out_specs=const(8, RP, 64 * KP),
        scratch_shapes=[
            pltpu.VMEM((RP, CHUNK), BF16),
            pltpu.VMEM((16, CHUNK), F32),
            pltpu.VMEM((2 * RP, CHUNK), BF16),
        ],
    )(place, a_irrep, occ, c_irrep.reshape(16, 32), spread, tile, pick, t_slab)
    t_got = lax.all_to_all(t_parts, "rep", split_axis=0, concat_axis=0, tiled=True)

    w_z = lax.all_to_all(
        jnp.broadcast_to(w_own[None], (ZS, KP, NP)), "idx", split_axis=0, concat_axis=0,
        axis_index_groups=Z_GROUPS, tiled=True,
    )
    w_all = lax.all_gather(w_z, "idx", axis=0, axis_index_groups=X_GROUPS)
    partial = call(
        mm_kernel, (8 * RP, NP), F32, [VMEM, VMEM], 2 * 256 * 2048 * 256, 2 * 10**6, out_specs=VMEM
    )(t_got.reshape(8 * RP, 64 * KP), w_all.reshape(64 * KP, NP))
    ends = lax.all_to_all(partial.reshape(8, RP, NP), "rep", split_axis=0, concat_axis=0, tiled=True)
    return call(
        end_kernel, (ROWS, 400), F32, [SMEM, SMEM, SMEM, SMEM, SMEM, VMEM, VMEM, VMEM], 10**6, 3 * 10**5,
        out_specs=VMEM,
    )(place, a_irrep, b_irrep, eps_a, eps_b, occ, eps_occ.reshape(1, O), ends)


def solution(mesh):
    in_specs = (P(("idx", "rep"), None), P(("idx", "rep"), None), P(), P(), P(), P(), P(), P(), P())
    out_specs = P(("idx", "rep"), None)
    return jax.shard_map(
        per_device, mesh=mesh, in_specs=in_specs, out_specs=out_specs, check_vma=False
    )
```

```python
import jax
import jax.numpy as jnp
from jax import lax
from jax.experimental import pallas as pl
from jax.experimental.pallas import tpu as pltpu
from jax.sharding import PartitionSpec as P

O = 100
G = 8
COLS = 400
KP = 64
NP = 128
RP = 32
ROWS = 25
GROUP = G * O
CHUNK = 4 * GROUP
CHUNKS = 16
STEP = 4
WINDOW = 896
F32, BF16, I32 = jnp.float32, jnp.bfloat16, jnp.int32
HBM = pl.BlockSpec(memory_space=pltpu.HBM)
ZS, XS, YS, CS = 16, 4, 4, 2
Z_GROUPS = [[x * ZS + z for z in range(ZS)] for x in range(XS)]
PLANES = [
    [(x * ZS + z) * YS * CS + p for x in range(XS) for p in range(YS * CS)] for z in range(ZS)
]


def iota(shape, dim):
    return lax.broadcasted_iota(I32, shape, dim)


def mod_o(n):
    return n - O * jnp.floor((n.astype(F32) + 0.5) * (1.0 / O)).astype(I32)


def to_rows(lanes, count, first):
    shape = (count, lanes.shape[1])
    hit = iota(shape, 1) == iota(shape, 0) + first
    return jnp.sum(jnp.where(hit, lanes, 0.0), axis=1, keepdims=True)


def tiled(lanes, width):
    rows = to_rows(lanes, 104, 0)
    hit = iota((104, width), 0) == mod_o(iota((1, width), 1))
    return jnp.sum(jnp.where(hit, rows, 0.0), axis=0, keepdims=True)


def by_slab(ref, dtype):
    s = iota((1, COLS), 1)
    out = jnp.full((1, COLS), ref[0], dtype)
    for b in range(1, COLS // O):
        out = jnp.where(s >= b * O, ref[b], out)
    return out


def place():
    return lax.axis_index("idx") * (YS * CS) + lax.axis_index("rep")


def fetch(sources, targets, sems):
    copies = [pltpu.make_async_copy(s, t, sems.at[i]) for i, (s, t) in enumerate(zip(sources, targets))]
    for copy in copies:
        copy.start()
    for copy in copies:
        copy.wait()


def w_kernel(c_hbm, b_hbm, occ_hbm, w_hbm, out_ref, c_irrep, b_irrep, occ, w_ref, flat, sems):
    fetch((c_hbm, b_hbm, occ_hbm, w_hbm), (c_irrep, b_irrep, occ, w_ref), sems)
    occ_f = occ[...].astype(F32)
    s = iota((COLS, 1), 0)
    slab = jnp.full((COLS, 1), b_irrep[0], I32)
    for b in range(1, COLS // O):
        slab = jnp.where(s >= b * O, b_irrep[b], slab)
    hit = iota((COLS, O), 1) == mod_o(s)
    col = slab ^ jnp.sum(jnp.where(hit, occ_f, 0.0), axis=1, keepdims=True).astype(I32)
    row = c_irrep[place()] ^ occ[...]
    flat[...] = jnp.zeros_like(flat)
    flat[:COLS, :O] = jnp.where(row == col, w_ref[...].astype(F32), 0.0)
    for n in range(4):
        part = flat[NP * n : NP * n + NP, :].T.astype(BF16)
        for half in range(2):
            out_ref[4 * half + n] = part[KP * half : KP * half + KP]


def t_kernel(
    a_hbm, c_hbm, occ_hbm, t_hbm, out_ref, a_irrep, c_lanes, occ, t_ref, want, have, pick, kept, sems, t_sems
):
    def block(q):
        lanes = pl.ds(CHUNK * q, CHUNK)
        return pltpu.make_async_copy(t_hbm.at[:, lanes], t_ref.at[:, lanes], t_sems.at[q])

    small = [
        pltpu.make_async_copy(s, t, sems.at[i])
        for i, (s, t) in enumerate(((a_hbm, a_irrep), (c_hbm, c_lanes), (occ_hbm, occ)))
    ]
    for copy in small:
        copy.start()
    for q in range(CHUNKS):
        block(q).start()
    for j in range(4):
        at = iota((WINDOW, 1), 0) - 32 * j
        k = jnp.where((at >= 0) & (at < GROUP), mod_o(jnp.maximum(at, 0)), -1)
        pick[j] = jnp.where(k == iota((WINDOW, 128), 1), 1.0, 0.0).astype(BF16)
    fold = jnp.where(iota((512, 128), 0) % 32 == iota((512, 128), 1), 1.0, 0.0).astype(BF16)
    lane = iota((128, CHUNK), 1)
    first = O * iota((128, 1), 0)
    spread = jnp.where((lane >= first) & (lane < first + O), 1.0, 0.0).astype(BF16)
    for q in range(CHUNKS):
        kept[RP * q + 16 : RP * q + RP, :] = jnp.zeros((16, CHUNK), BF16)
    for copy in small:
        copy.wait()
    here = place()
    occ_f = occ[...].astype(F32)
    row = a_irrep[here // 4] ^ to_rows(occ_f, RP, ROWS * (here % 4)).astype(I32)
    want[...] = (row ^ tiled(occ_f, CHUNK).astype(I32)).astype(BF16)
    shape = (CHUNKS, 512)
    mine = jnp.where(iota(shape, 1) // 32 == iota(shape, 0), c_lanes[...].astype(F32), 0.0)
    rows = jnp.dot(mine.astype(BF16), fold, preferred_element_type=F32).astype(BF16)
    have[...] = jnp.dot(rows, spread, preferred_element_type=F32)
    for q in range(CHUNKS):
        block(q).wait()
        mask = want[:ROWS, :] == have[q : q + 1, :].astype(BF16)
        got = t_ref[:, CHUNK * q : CHUNK * (q + 1)]
        kept[RP * q : RP * q + ROWS, :] = jnp.where(mask, got, jnp.zeros((), BF16))
    low = iota((CHUNKS * RP, 128), 1) < KP
    for pair in range(2):
        even, odd = (
            jnp.dot(kept[:, 768 * j : 768 * j + WINDOW], pick[j], preferred_element_type=F32)
            for j in (2 * pair, 2 * pair + 1)
        )
        halves = (
            jnp.where(low, even, pltpu.roll(odd, KP, 1)),
            jnp.where(low, pltpu.roll(even, KP, 1), odd),
        )
        for half in range(2):
            packed = halves[half].astype(BF16)
            for q in range(CHUNKS):
                x, h = divmod(q, CHUNKS // XS)
                lanes = slice(256 * h + 128 * pair, 256 * h + 128 * pair + 128)
                part = packed[RP * q : RP * q + RP]
                for n in range(4):
                    out_ref[YS * CS * x + 4 * half + n, :, lanes] = part


def mm_kernel(
    t_ref, w_ref, a_hbm, b_hbm, ea_hbm, eb_hbm, occ_hbm, eo_hbm, out_ref, energy_ref, same_ref,
    a_irrep, b_irrep, eps_a, eps_b, occ, eps_occ, sems
):
    copies = [
        pltpu.make_async_copy(s, t, sems.at[i])
        for i, (s, t) in enumerate(
            zip((a_hbm, b_hbm, ea_hbm, eb_hbm, occ_hbm, eo_hbm), (a_irrep, b_irrep, eps_a, eps_b, occ, eps_occ))
        )
    ]
    for copy in copies:
        copy.start()
    out_ref[...] = jnp.dot(t_ref[...], w_ref[...], preferred_element_type=F32)
    for copy in copies:
        copy.wait()
    here = place()
    first = ROWS * (here % 4)
    a = here // 4
    occ_f, eo = occ[...].astype(F32), eps_occ[...]
    row = a_irrep[a] ^ to_rows(occ_f, ROWS, first).astype(I32)
    col = by_slab(b_irrep, I32) ^ tiled(occ_f, COLS).astype(I32)
    energy_ref[...] = (eps_a[a] - to_rows(eo, ROWS, first)) + (by_slab(eps_b, F32) - tiled(eo, COLS))
    same_ref[...] = jnp.where(row == col, 1.0, 0.0)


def end_kernel(energy_ref, same_ref, part_ref, out_ref):
    for n in range(4):
        lo, hi = NP * n, min(NP * n + NP, COLS)
        total = None
        for x in range(XS):
            for half in range(2):
                part = part_ref[YS * CS * x + 4 * half + n, :ROWS, : hi - lo]
                total = part if total is None else total + part
        total = jnp.where(same_ref[:, lo:hi] > 0.5, total, 0.0)
        out_ref[:, lo:hi] = total / energy_ref[:, lo:hi]


def call(kernel, shape, dtype, flops, moved, room=48, **rest):
    return pl.pallas_call(
        kernel,
        out_shape=(
            [jax.ShapeDtypeStruct(one, dtype) for one in shape]
            if isinstance(shape, list)
            else jax.ShapeDtypeStruct(shape, dtype)
        ),
        cost_estimate=pl.CostEstimate(flops=flops, bytes_accessed=moved, transcendentals=0),
        compiler_params=pltpu.CompilerParams(vmem_limit_bytes=room * 2**20),
        **rest,
    )


def per_device(t_slab, w_cycle, a_irrep, b_irrep, c_irrep, occ_irrep, eps_a, eps_b, eps_occ):
    vmem, smem, dma = pltpu.VMEM, pltpu.SMEM, pltpu.SemaphoreType.DMA
    whole = pl.BlockSpec(memory_space=pltpu.VMEM)
    occ, eo = occ_irrep.reshape(1, O), eps_occ.reshape(1, O)
    w_parts = call(
        w_kernel, (8, KP, NP), BF16, 10**6, 2 * 10**5, room=58,
        in_specs=[HBM] * 4,
        out_specs=whole,
        scratch_shapes=[
            smem((512,), I32), smem((4,), I32), vmem((1, O), I32), vmem((COLS, O), BF16),
            vmem((4 * NP, 2 * KP), F32), dma((4,)),
        ],
    )(c_irrep, b_irrep, occ, w_cycle.T)
    occ_late, w_parts = lax.optimization_barrier((occ, w_parts))
    w_got = lax.all_to_all(w_parts, "rep", split_axis=0, concat_axis=0, tiled=True)
    w_own = jnp.sum(w_got, axis=0, dtype=BF16)
    t_parts = call(
        t_kernel, (XS * YS * CS, RP, 16 * KP), BF16, 4 * 10**9, 4 * 10**6, room=58,
        in_specs=[HBM] * 4,
        out_specs=whole,
        scratch_shapes=[
            smem((128,), I32),
            vmem((1, 512), I32),
            vmem((1, O), I32),
            vmem((ROWS, CHUNKS * CHUNK), BF16),
            vmem((RP, CHUNK), BF16),
            vmem((CHUNKS, CHUNK), F32),
            vmem((4, WINDOW, 128), BF16),
            vmem((CHUNKS * RP, CHUNK), BF16),
            dma((3,)),
            dma((CHUNKS,)),
        ],
    )(a_irrep, c_irrep.reshape(1, 512), occ_late, t_slab)
    t_got = lax.all_to_all(
        t_parts, ("idx", "rep"), split_axis=0, concat_axis=0, axis_index_groups=PLANES, tiled=True
    )

    w_own, t_parts = lax.optimization_barrier((w_own, t_parts))
    w_z = lax.all_gather(w_own, "idx", axis=0, axis_index_groups=Z_GROUPS)
    partial, energy, same = call(
        mm_kernel, [(XS * YS * CS * RP, NP), (ROWS, COLS), (ROWS, COLS)], F32, 2 * 1024 * 1024 * 128, 3 * 10**6, room=24,
        in_specs=[whole] * 2 + [HBM] * 6,
        out_specs=[whole] * 3,
        scratch_shapes=[
            smem((128,), I32), smem((4,), I32), smem((128,), F32), smem((4,), F32),
            vmem((1, O), I32), vmem((1, O), F32), dma((6,)),
        ],
    )(t_got.reshape(-1, 16 * KP), w_z.reshape(ZS * KP, NP), a_irrep, b_irrep, eps_a, eps_b, occ, eo)
    ends = lax.all_to_all(
        partial.reshape(-1, RP, NP), ("idx", "rep"), split_axis=0, concat_axis=0,
        axis_index_groups=PLANES, tiled=True,
    )
    return call(
        end_kernel, (ROWS, COLS), F32, 10**6, 10**6, room=24, in_specs=[whole] * 3, out_specs=whole
    )(energy, same, ends)


def solution(mesh):
    in_specs = (P(("idx", "rep"), None), P(("idx", "rep"), None), P(), P(), P(), P(), P(), P(), P())
    out_specs = P(("idx", "rep"), None)
    return jax.shard_map(
        per_device, mesh=mesh, in_specs=in_specs, out_specs=out_specs, check_vma=False
    )
```

```python
import jax
import jax.numpy as jnp
from jax import lax
from jax.experimental import pallas as pl
from jax.experimental.pallas import tpu as pltpu
from jax.sharding import PartitionSpec as P

O = 100
G = 8
COLS = 400
NP = 128
KP = 128
RP = 32
ROWS = 25
GROUP = G * O
CHUNK = 4 * GROUP
CHUNKS = 16
PER_X = 4
WINDOW = 896
F32, BF16, I32 = jnp.float32, jnp.bfloat16, jnp.int32
HBM = pl.BlockSpec(memory_space=pltpu.HBM)
ZS, XS, YS, CS = 16, 4, 4, 2
Z_GROUPS = [[x * ZS + z for z in range(ZS)] for x in range(XS)]
CORE_PLANES = [
    [(x * ZS + z) * YS * CS + y * CS + c for x in range(XS) for y in range(YS)]
    for z in range(ZS)
    for c in range(CS)
]
Z_CORE_GROUPS = [
    [(x * ZS + z) * YS * CS + y * CS + c for z in range(ZS) for c in range(CS)]
    for x in range(XS)
    for y in range(YS)
]


def iota(shape, dim):
    return lax.broadcasted_iota(I32, shape, dim)


def mod_o(n):
    return n - O * jnp.floor((n.astype(F32) + 0.5) * (1.0 / O)).astype(I32)


def to_rows(lanes, count, first):
    shape = (count, lanes.shape[1])
    hit = iota(shape, 1) == iota(shape, 0) + first
    return jnp.sum(jnp.where(hit, lanes, 0.0), axis=1, keepdims=True)


def tiled(lanes, width):
    rows = to_rows(lanes, 104, 0)
    hit = iota((104, width), 0) == mod_o(iota((1, width), 1))
    return jnp.sum(jnp.where(hit, rows, 0.0), axis=0, keepdims=True)


def by_slab(ref, dtype):
    s = iota((1, COLS), 1)
    out = jnp.full((1, COLS), ref[0], dtype)
    for b in range(1, COLS // O):
        out = jnp.where(s >= b * O, ref[b], out)
    return out


def place():
    return lax.axis_index("idx") * (YS * CS) + lax.axis_index("rep")


def fetch(sources, targets, sems):
    copies = [pltpu.make_async_copy(s, t, sems.at[i]) for i, (s, t) in enumerate(zip(sources, targets))]
    for copy in copies:
        copy.start()
    for copy in copies:
        copy.wait()


def w_kernel(c_hbm, b_hbm, occ_hbm, w_hbm, out_ref, c_irrep, b_irrep, occ, w_ref, sems):
    fetch((c_hbm, b_hbm, occ_hbm, w_hbm), (c_irrep, b_irrep, occ, w_ref), sems)
    s = iota((COLS, 1), 0)
    slab = jnp.full((COLS, 1), b_irrep[0], I32)
    for b in range(1, COLS // O):
        slab = jnp.where(s >= b * O, b_irrep[b], slab)
    hit = iota((COLS, O), 1) == mod_o(s)
    col = slab ^ jnp.sum(jnp.where(hit, occ[...].astype(F32), 0.0), axis=1, keepdims=True).astype(I32)
    row = c_irrep[place()] ^ occ[...]
    out_ref[...] = jnp.zeros_like(out_ref)
    out_ref[:COLS, :O] = jnp.where(row == col, w_ref[...].astype(F32), 0.0).astype(BF16)


def t_kernel(
    a_hbm, c_hbm, occ_hbm, t_hbm, out_hbm, a_irrep, c_lanes, occ, t_ref, want, have, pick, kept, packed, sems, t_sems, o_sems
):
    def block(q):
        lanes = pl.ds(CHUNK * q, CHUNK)
        return pltpu.make_async_copy(t_hbm.at[:, lanes], t_ref.at[:, lanes], t_sems.at[q])

    def send(x, y):
        return pltpu.make_async_copy(packed.at[x], out_hbm.at[YS * x + y], o_sems.at[YS * x + y])

    small = [
        pltpu.make_async_copy(s, t, sems.at[i])
        for i, (s, t) in enumerate(((a_hbm, a_irrep), (c_hbm, c_lanes), (occ_hbm, occ)))
    ]
    for copy in small:
        copy.start()
    for q in range(CHUNKS):
        block(q).start()
    for j in range(4):
        at = iota((WINDOW, 1), 0) - 32 * j
        k = jnp.where((at >= 0) & (at < GROUP), mod_o(jnp.maximum(at, 0)), -1)
        pick[j] = jnp.where(k == iota((WINDOW, KP), 1), 1.0, 0.0).astype(BF16)
    fold = jnp.where(iota((512, 128), 0) % 32 == iota((512, 128), 1), 1.0, 0.0).astype(BF16)
    lane = iota((128, CHUNK), 1)
    first = O * iota((128, 1), 0)
    spread = jnp.where((lane >= first) & (lane < first + O), 1.0, 0.0).astype(BF16)
    for q in range(CHUNKS):
        kept[RP * q + 16 : RP * q + RP, :] = jnp.zeros((16, CHUNK), BF16)
    for copy in small:
        copy.wait()
    here = place()
    occ_f = occ[...].astype(F32)
    row = a_irrep[here // 4] ^ to_rows(occ_f, RP, ROWS * (here % 4)).astype(I32)
    want[...] = (row ^ tiled(occ_f, CHUNK).astype(I32)).astype(BF16)
    shape = (CHUNKS, 512)
    mine = jnp.where(iota(shape, 1) // 32 == iota(shape, 0), c_lanes[...].astype(F32), 0.0)
    rows = jnp.dot(mine.astype(BF16), fold, preferred_element_type=F32).astype(BF16)
    have[...] = jnp.dot(rows, spread, preferred_element_type=F32)
    for x in range(XS):
        part = slice(RP * PER_X * x, RP * PER_X * (x + 1))
        for q in range(PER_X * x, PER_X * (x + 1)):
            block(q).wait()
            mask = want[:ROWS, :] == have[q : q + 1, :].astype(BF16)
            got = t_ref[:, CHUNK * q : CHUNK * (q + 1)]
            kept[RP * q : RP * q + ROWS, :] = jnp.where(mask, got, jnp.zeros((), BF16))
        for j in range(4):
            full = jnp.dot(kept[part, 768 * j : 768 * j + WINDOW], pick[j], preferred_element_type=F32)
            for h in range(PER_X):
                lanes = slice(KP * (4 * h + j), KP * (4 * h + j + 1))
                packed[x, :, lanes] = full[RP * h : RP * (h + 1)].astype(BF16)
        for y in range(YS):
            send(x, y).start()
    for x in range(XS):
        for y in range(YS):
            send(x, y).wait()


def mm_kernel(
    t_ref, w_ref, a_hbm, b_hbm, ea_hbm, eb_hbm, occ_hbm, eo_hbm, out_ref, energy_ref, same_ref,
    a_irrep, b_irrep, eps_a, eps_b, occ, eps_occ, sems
):
    copies = [
        pltpu.make_async_copy(s, t, sems.at[i])
        for i, (s, t) in enumerate(
            zip((a_hbm, b_hbm, ea_hbm, eb_hbm, occ_hbm, eo_hbm), (a_irrep, b_irrep, eps_a, eps_b, occ, eps_occ))
        )
    ]
    for copy in copies:
        copy.start()
    w_t = jnp.concatenate([w_ref[z] for z in range(ZS)], axis=1)
    out_ref[...] = lax.dot_general(
        t_ref[...], w_t, (((1,), (1,)), ((), ())), preferred_element_type=F32
    )
    for copy in copies:
        copy.wait()
    here = place()
    first = ROWS * (here % 4)
    a = here // 4
    occ_f, eo = occ[...].astype(F32), eps_occ[...]
    row = a_irrep[a] ^ to_rows(occ_f, ROWS, first).astype(I32)
    col = by_slab(b_irrep, I32) ^ tiled(occ_f, COLS).astype(I32)
    energy_ref[...] = (eps_a[a] - to_rows(eo, ROWS, first)) + (by_slab(eps_b, F32) - tiled(eo, COLS))
    same_ref[...] = jnp.where(row == col, 1.0, 0.0)


def end_kernel(energy_ref, same_ref, part_ref, out_ref):
    for n in range(4):
        lo, hi = NP * n, min(NP * n + NP, COLS)
        total = part_ref[n, :ROWS, : hi - lo]
        for x in range(1, XS):
            total = total + part_ref[YS * x + n, :ROWS, : hi - lo]
        total = jnp.where(same_ref[:, lo:hi] > 0.5, total, 0.0)
        out_ref[:, lo:hi] = total / energy_ref[:, lo:hi]


def call(kernel, shape, dtype, flops, moved, room=48, **rest):
    return pl.pallas_call(
        kernel,
        out_shape=(
            [jax.ShapeDtypeStruct(one, dtype) for one in shape]
            if isinstance(shape, list)
            else jax.ShapeDtypeStruct(shape, dtype)
        ),
        cost_estimate=pl.CostEstimate(flops=flops, bytes_accessed=moved, transcendentals=0),
        compiler_params=pltpu.CompilerParams(vmem_limit_bytes=room * 2**20),
        **rest,
    )


def per_device(t_slab, w_cycle, a_irrep, b_irrep, c_irrep, occ_irrep, eps_a, eps_b, eps_occ):
    vmem, smem, dma = pltpu.VMEM, pltpu.SMEM, pltpu.SemaphoreType.DMA
    whole = pl.BlockSpec(memory_space=pltpu.VMEM)
    occ, eo = occ_irrep.reshape(1, O), eps_occ.reshape(1, O)
    w_parts = call(
        w_kernel, (4 * NP, KP), BF16, 10**6, 2 * 10**5, room=58,
        in_specs=[HBM] * 4,
        out_specs=whole,
        scratch_shapes=[smem((512,), I32), smem((4,), I32), vmem((1, O), I32), vmem((COLS, O), BF16), dma((4,))],
    )(c_irrep, b_irrep, occ, w_cycle.T)
    occ_late, w_parts = lax.optimization_barrier((occ, w_parts))
    w_parts = w_parts.reshape(8, NP // 2, KP)
    w_got = lax.all_to_all(w_parts, "rep", split_axis=0, concat_axis=0, tiled=True)
    w_own = jnp.sum(w_got, axis=0, dtype=BF16)
    t_parts = call(
        t_kernel, (XS * YS, RP, ZS * KP), BF16, 4 * 10**9, 4 * 10**6, room=58,
        in_specs=[HBM] * 4,
        out_specs=HBM,
        scratch_shapes=[
            smem((128,), I32),
            vmem((1, 512), I32),
            vmem((1, O), I32),
            vmem((ROWS, CHUNKS * CHUNK), BF16),
            vmem((RP, CHUNK), BF16),
            vmem((CHUNKS, CHUNK), F32),
            vmem((4, WINDOW, KP), BF16),
            vmem((CHUNKS * RP, CHUNK), BF16),
            vmem((XS, RP, ZS * KP), BF16),
            dma((3,)),
            dma((CHUNKS,)),
            dma((XS * YS,)),
        ],
    )(a_irrep, c_irrep.reshape(1, 512), occ_late, t_slab)
    t_got = lax.all_to_all(
        t_parts, ("idx", "rep"), split_axis=0, concat_axis=0, axis_index_groups=CORE_PLANES, tiled=True
    )

    w_own, t_parts = lax.optimization_barrier((w_own, t_parts))
    w_z = lax.all_gather(w_own, ("idx", "rep"), axis=0, axis_index_groups=Z_CORE_GROUPS)
    partial, energy, same = call(
        mm_kernel, [(XS * YS * RP, NP), (ROWS, COLS), (ROWS, COLS)], F32, 2 * 512 * 2048 * 128, 3 * 10**6, room=24,
        in_specs=[whole] * 2 + [HBM] * 6,
        out_specs=[whole] * 3,
        scratch_shapes=[
            smem((128,), I32), smem((4,), I32), smem((128,), F32), smem((4,), F32),
            vmem((1, O), I32), vmem((1, O), F32), dma((6,)),
        ],
    )(t_got.reshape(-1, ZS * KP), w_z.reshape(ZS, NP, KP), a_irrep, b_irrep, eps_a, eps_b, occ, eo)
    ends = lax.all_to_all(
        partial.reshape(-1, RP, NP), ("idx", "rep"), split_axis=0, concat_axis=0,
        axis_index_groups=CORE_PLANES, tiled=True,
    )
    return call(
        end_kernel, (ROWS, COLS), F32, 10**6, 10**6, room=24, in_specs=[whole] * 3, out_specs=whole
    )(energy, same, ends)


def solution(mesh):
    in_specs = (P(("idx", "rep"), None), P(("idx", "rep"), None), P(), P(), P(), P(), P(), P(), P())
    out_specs = P(("idx", "rep"), None)
    return jax.shard_map(
        per_device, mesh=mesh, in_specs=in_specs, out_specs=out_specs, check_vma=False
    )
```

```python
import jax
import jax.numpy as jnp
from jax import lax
from jax.experimental import pallas as pl
from jax.experimental.pallas import tpu as pltpu
from jax.sharding import PartitionSpec as P

O = 100
G = 8
COLS = 400
NP = 128
KP = 128
RP = 32
ROWS = 25
GROUP = G * O
CHUNK = 4 * GROUP
CHUNKS = 16
PER_X = 4
WINDOW = 896
F32, BF16, I32 = jnp.float32, jnp.bfloat16, jnp.int32
HBM = pl.BlockSpec(memory_space=pltpu.HBM)
ZS, XS, YS, CS = 16, 4, 4, 2
Z_GROUPS = [[x * ZS + z for z in range(ZS)] for x in range(XS)]
CORE_PLANES = [
    [(x * ZS + z) * YS * CS + y * CS + c for x in range(XS) for y in range(YS)]
    for z in range(ZS)
    for c in range(CS)
]
Z_CORE_GROUPS = [
    [(x * ZS + z) * YS * CS + y * CS + c for z in range(ZS) for c in range(CS)]
    for x in range(XS)
    for y in range(YS)
]


def iota(shape, dim):
    return lax.broadcasted_iota(I32, shape, dim)


def mod_o(n):
    return n - O * jnp.floor((n.astype(F32) + 0.5) * (1.0 / O)).astype(I32)


def to_rows(lanes, count, first):
    shape = (count, lanes.shape[1])
    hit = iota(shape, 1) == iota(shape, 0) + first
    return jnp.sum(jnp.where(hit, lanes, 0.0), axis=1, keepdims=True)


def lookup(lanes, index):
    parts = [
        jnp.take_along_axis(lanes, index[:, at : at + 128], axis=1) for at in range(0, index.shape[1], 128)
    ]
    return jnp.concatenate(parts, axis=1)


def by_slab(ref, dtype):
    s = iota((8, 4 * NP), 1)
    out = jnp.full((8, 4 * NP), ref[0, 0], dtype)
    for b in range(1, COLS // O):
        out = jnp.where(s >= b * O, ref[0, b], out)
    return out


def fetch(sources, targets, sems):
    copies = [pltpu.make_async_copy(s, t, sems.at[i]) for i, (s, t) in enumerate(zip(sources, targets))]
    for copy in copies:
        copy.start()
    return copies


def place():
    return lax.axis_index("idx") * (YS * CS) + lax.axis_index("rep")


def padded(lanes):
    wide = jnp.concatenate([lanes, jnp.zeros((1, 128 - O), lanes.dtype)], axis=1)
    return jnp.broadcast_to(wide, (8, 128))


def head_kernel(b_hbm, c_hbm, occ_hbm, w_hbm, t_hbm, out_hbm, t_ref, b_irrep, c_irrep, occ, w_ref, out_ref, sems, t_sem, out_sem):
    copies = fetch((b_hbm, c_hbm, occ_hbm, w_hbm), (b_irrep, c_irrep, occ, w_ref), sems)
    whole_t = pltpu.make_async_copy(t_hbm, t_ref, t_sem)
    whole_t.start()
    out_ref[...] = jnp.zeros_like(out_ref)
    s = iota((COLS, 1), 0)
    hit = iota((COLS, O), 1) == mod_o(s)
    for copy in copies:
        copy.wait()
    slab = jnp.full((COLS, 1), b_irrep[0, 0], I32)
    for b in range(1, COLS // O):
        slab = jnp.where(s >= b * O, b_irrep[0, b], slab)
    col = slab ^ jnp.sum(jnp.where(hit, occ[...].astype(F32), 0.0), axis=1, keepdims=True).astype(I32)
    row = c_irrep[0, place()] ^ occ[...]
    out_ref[:COLS, :O] = jnp.where(row == col, w_ref[...].astype(F32), 0.0).astype(BF16)
    send = pltpu.make_async_copy(out_ref, out_hbm, out_sem)
    send.start()
    send.wait()
    whole_t.wait()


def t_kernel(
    a_hbm, c_hbm, occ_hbm, b_hbm, ea_hbm, eb_hbm, eo_hbm, t_ref, out_hbm, energy, same,
    a_irrep, c_lanes, occ, b_irrep, eps_a, eps_b, eps_occ, want, have, pick, kept, packed, sems, o_sems,
):
    def send(x, y):
        return pltpu.make_async_copy(packed.at[x], out_hbm.at[YS * x + y], o_sems.at[YS * x + y])

    copies = fetch(
        (a_hbm, c_hbm, occ_hbm, b_hbm, ea_hbm, eb_hbm, eo_hbm),
        (a_irrep, c_lanes, occ, b_irrep, eps_a, eps_b, eps_occ),
        sems,
    )
    at = iota((WINDOW + 96, 1), 0) - 96
    k = jnp.where((at >= 0) & (at < GROUP), mod_o(jnp.maximum(at, 0)), -1)
    pick[...] = jnp.where(k == iota((WINDOW + 96, KP), 1), 1.0, 0.0).astype(BF16)
    for q in range(CHUNKS):
        kept[RP * q + 16 : RP * q + RP, :] = jnp.zeros((16, CHUNK), BF16)
    lane = iota((8, CHUNK), 1)
    mod = mod_o(lane)
    over = (lane - mod) // O
    group = iota((8, 128), 0) // 4
    for copy in copies:
        copy.wait()
    here = place()
    a, first = here // 4, ROWS * (here % 4)
    row = a_irrep[0, a] ^ to_rows(occ[...].astype(F32), RP, first).astype(I32)
    occ_t = lookup(padded(occ[...]), mod)
    want[...] = (row ^ occ_t[:1]).astype(BF16)
    for half in range(2):
        lanes = [jnp.broadcast_to(c_lanes[:, 128 * v : 128 * v + 128], (8, 128)) for v in (2 * half, 2 * half + 1)]
        source = jnp.where(group == 0, lanes[0], lanes[1])
        have[8 * half : 8 * half + 8, :] = lookup(source, 32 * (iota((8, CHUNK), 0) % 4) + over).astype(F32)
    for x in range(XS):
        part = slice(RP * PER_X * x, RP * PER_X * (x + 1))
        for q in range(PER_X * x, PER_X * (x + 1)):
            mask = want[:ROWS, :] == have[q : q + 1, :].astype(BF16)
            got = t_ref[:, CHUNK * q : CHUNK * (q + 1)]
            kept[RP * q : RP * q + ROWS, :] = jnp.where(mask, got, jnp.zeros((), BF16))
        for j in range(4):
            full = jnp.dot(
                kept[part, 768 * j : 768 * j + WINDOW],
                pick[96 - 32 * j : 96 - 32 * j + WINDOW, :],
                preferred_element_type=F32,
            )
            for h in range(PER_X):
                lanes = slice(KP * (4 * h + j), KP * (4 * h + j + 1))
                packed[x, :, lanes] = full[RP * h : RP * (h + 1)].astype(BF16)
        for y in range(YS):
            send(x, y).start()
    wide = 4 * NP
    col = (by_slab(b_irrep, I32) ^ occ_t[:, :wide])[:1, :COLS]
    column_energy = (by_slab(eps_b, F32) - lookup(padded(eps_occ[...]), mod[:, :wide]))[:1, :COLS]
    energy[...] = (eps_a[0, a] - to_rows(eps_occ[...], ROWS, first)) + column_energy
    same[...] = jnp.where(row[:ROWS] == col, 1.0, 0.0)
    for x in range(XS):
        for y in range(YS):
            send(x, y).wait()


def mm_kernel(t_ref, w_ref, out_ref):
    w_t = jnp.concatenate([w_ref[z] for z in range(ZS)], axis=1)
    out_ref[...] = lax.dot_general(
        t_ref[...], w_t, (((1,), (1,)), ((), ())), preferred_element_type=F32
    )


def end_kernel(energy_ref, same_ref, part_ref, out_ref):
    for n in range(4):
        lo, hi = NP * n, min(NP * n + NP, COLS)
        total = part_ref[n, :ROWS, : hi - lo]
        for x in range(1, XS):
            total = total + part_ref[YS * x + n, :ROWS, : hi - lo]
        total = jnp.where(same_ref[:, lo:hi] > 0.5, total, 0.0)
        out_ref[:, lo:hi] = total / energy_ref[:, lo:hi]


def call(kernel, out, flops, moved, room, **rest):
    return pl.pallas_call(
        kernel,
        out_shape=out,
        cost_estimate=pl.CostEstimate(flops=flops, bytes_accessed=moved, transcendentals=0),
        compiler_params=pltpu.CompilerParams(vmem_limit_bytes=room * 2**20),
        **rest,
    )


def per_device(t_slab, w_cycle, a_irrep, b_irrep, c_irrep, occ_irrep, eps_a, eps_b, eps_occ):
    vmem, smem, dma = pltpu.VMEM, pltpu.SMEM, pltpu.SemaphoreType.DMA
    struct = jax.ShapeDtypeStruct
    whole = pl.BlockSpec(memory_space=pltpu.VMEM)
    lanes = lambda vector: vector.reshape(1, -1)
    a_row, b_row, c_row, occ, eo = (lanes(v) for v in (a_irrep, b_irrep, c_irrep, occ_irrep, eps_occ))
    w_parts, t_near = call(
        head_kernel,
        [pltpu.HBM((4 * NP, KP), BF16), vmem((ROWS, CHUNKS * CHUNK), BF16)],
        10**7, 10**6, 56,
        in_specs=[HBM] * 5,
        out_specs=[HBM, whole],
        scratch_shapes=[
            smem((1, 4), I32), smem((1, 512), I32), vmem((1, O), I32), vmem((COLS, O), BF16),
            vmem((4 * NP, KP), BF16), dma((4,)), dma, dma,
        ],
    )(b_row, c_row, occ, w_cycle.T, t_slab)
    w_got = lax.all_to_all(w_parts.reshape(8, NP // 2, KP), "rep", split_axis=0, concat_axis=0, tiled=True)
    w_own = jnp.sum(w_got, axis=0, dtype=BF16)
    t_parts, energy, same = call(
        t_kernel,
        [pltpu.HBM((XS * YS, RP, ZS * KP), BF16), struct((ROWS, COLS), F32), struct((ROWS, COLS), F32)],
        4 * 10**9, 4 * 10**6, 55,
        in_specs=[HBM] * 7 + [whole],
        out_specs=[HBM, whole, whole],
        scratch_shapes=[
            smem((1, 128), I32), vmem((1, 512), I32), vmem((1, O), I32), smem((1, 4), I32), smem((1, 128), F32),
            smem((1, 4), F32), vmem((1, O), F32), vmem((RP, CHUNK), BF16), vmem((CHUNKS, CHUNK), F32),
            vmem((WINDOW + 96, KP), BF16), vmem((CHUNKS * RP, CHUNK), BF16), vmem((XS, RP, ZS * KP), BF16),
            dma((7,)), dma((XS * YS,)),
        ],
    )(
        a_row, c_row, occ, b_row, lanes(eps_a), lanes(eps_b), eo,
        pltpu.with_memory_space_constraint(t_near, pltpu.VMEM),
    )
    t_got = lax.all_to_all(
        t_parts, ("idx", "rep"), split_axis=0, concat_axis=0, axis_index_groups=CORE_PLANES, tiled=True
    )
    w_own, t_parts = lax.optimization_barrier((w_own, t_parts))
    w_z = lax.all_gather(w_own, ("idx", "rep"), axis=0, axis_index_groups=Z_CORE_GROUPS)
    partial = call(
        mm_kernel, struct((XS * YS * RP, NP), F32), 2 * 512 * 2048 * 128, 3 * 10**6, 24,
        in_specs=[whole] * 2, out_specs=whole,
    )(t_got.reshape(-1, ZS * KP), w_z.reshape(ZS, NP, KP))
    ends = lax.all_to_all(
        partial.reshape(-1, RP, NP), ("idx", "rep"), split_axis=0, concat_axis=0,
        axis_index_groups=CORE_PLANES, tiled=True,
    )
    return call(
        end_kernel, struct((ROWS, COLS), F32), 10**6, 10**6, 24, in_specs=[whole] * 3, out_specs=whole
    )(energy, same, ends)


def solution(mesh):
    in_specs = (P(("idx", "rep"), None), P(("idx", "rep"), None), P(), P(), P(), P(), P(), P(), P())
    out_specs = P(("idx", "rep"), None)
    return jax.shard_map(
        per_device, mesh=mesh, in_specs=in_specs, out_specs=out_specs, check_vma=False
    )
```

```python
import jax
import jax.numpy as jnp
from jax import lax
from jax.experimental import pallas as pl
from jax.experimental.pallas import tpu as pltpu
from jax.sharding import PartitionSpec as P

O = 100
G = 8
COLS = 400
NP = 128
KP = 128
RP = 32
ROWS = 25
GROUP = G * O
CHUNK = 4 * GROUP
CHUNKS = 16
PER_X = 4
EARLY = CHUNKS // 2 * CHUNK
WINDOW = 896
F32, BF16, I32 = jnp.float32, jnp.bfloat16, jnp.int32
HBM = pl.BlockSpec(memory_space=pltpu.HBM)
ZS, XS, YS, CS = 16, 4, 4, 2
Z_GROUPS = [[x * ZS + z for z in range(ZS)] for x in range(XS)]
CORE_PLANES = [
    [(x * ZS + z) * YS * CS + y * CS + c for x in range(XS) for y in range(YS)]
    for z in range(ZS)
    for c in range(CS)
]
Z_CORE_GROUPS = [
    [(x * ZS + z) * YS * CS + y * CS + c for z in range(ZS) for c in range(CS)]
    for x in range(XS)
    for y in range(YS)
]


def iota(shape, dim):
    return lax.broadcasted_iota(I32, shape, dim)


def mod_o(n):
    return n - O * jnp.floor((n.astype(F32) + 0.5) * (1.0 / O)).astype(I32)


def to_rows(lanes, count, first):
    shape = (count, lanes.shape[1])
    hit = iota(shape, 1) == iota(shape, 0) + first
    return jnp.sum(jnp.where(hit, lanes, 0.0), axis=1, keepdims=True)


def lookup(lanes, index):
    parts = [
        jnp.take_along_axis(lanes, index[:, at : at + 128], axis=1) for at in range(0, index.shape[1], 128)
    ]
    return jnp.concatenate(parts, axis=1)


def by_slab(ref, dtype):
    s = iota((8, 4 * NP), 1)
    out = jnp.full((8, 4 * NP), ref[0, 0], dtype)
    for b in range(1, COLS // O):
        out = jnp.where(s >= b * O, ref[0, b], out)
    return out


def fetch(sources, targets, sems):
    copies = [pltpu.make_async_copy(s, t, sems.at[i]) for i, (s, t) in enumerate(zip(sources, targets))]
    for copy in copies:
        copy.start()
    return copies


def place():
    return lax.axis_index("idx") * (YS * CS) + lax.axis_index("rep")


def padded(lanes):
    wide = jnp.concatenate([lanes, jnp.zeros((1, 128 - O), lanes.dtype)], axis=1)
    return jnp.broadcast_to(wide, (8, 128))


def head_kernel(
    b_hbm, c_hbm, occ_hbm, w_hbm, t_hbm, out_hbm, t_ref, b_irrep, c_irrep, occ, w_ref, out_ref, sems, t_sem, out_sem
):
    copies = fetch((b_hbm, c_hbm, occ_hbm, w_hbm), (b_irrep, c_irrep, occ, w_ref), sems)
    early = pltpu.make_async_copy(t_hbm.at[:, pl.ds(0, EARLY)], t_ref, t_sem)
    early.start()
    out_ref[...] = jnp.zeros_like(out_ref)
    s = iota((COLS, 1), 0)
    hit = iota((COLS, O), 1) == mod_o(s)
    for copy in copies:
        copy.wait()
    slab = jnp.full((COLS, 1), b_irrep[0, 0], I32)
    for b in range(1, COLS // O):
        slab = jnp.where(s >= b * O, b_irrep[0, b], slab)
    col = slab ^ jnp.sum(jnp.where(hit, occ[...].astype(F32), 0.0), axis=1, keepdims=True).astype(I32)
    row = c_irrep[0, place()] ^ occ[...]
    out_ref[:COLS, :O] = jnp.where(row == col, w_ref[...].astype(F32), 0.0).astype(BF16)
    send = pltpu.make_async_copy(out_ref, out_hbm, out_sem)
    send.start()
    send.wait()
    early.wait()


def t_kernel(
    a_hbm, c_hbm, occ_hbm, b_hbm, ea_hbm, eb_hbm, eo_hbm, early, t_hbm, out_hbm, energy, same,
    a_irrep, c_lanes, occ, b_irrep, eps_a, eps_b, eps_occ, late, want, have, pick, kept, packed, sems, t_sem, o_sems,
):
    def send(x, y):
        return pltpu.make_async_copy(packed.at[x], out_hbm.at[YS * x + y], o_sems.at[YS * x + y])

    copies = fetch(
        (a_hbm, c_hbm, occ_hbm, b_hbm, ea_hbm, eb_hbm, eo_hbm),
        (a_irrep, c_lanes, occ, b_irrep, eps_a, eps_b, eps_occ),
        sems,
    )
    rest = pltpu.make_async_copy(t_hbm.at[:, pl.ds(EARLY, EARLY)], late, t_sem)
    rest.start()
    at = iota((WINDOW + 96, 1), 0) - 96
    k = jnp.where((at >= 0) & (at < GROUP), mod_o(jnp.maximum(at, 0)), -1)
    pick[...] = jnp.where(k == iota((WINDOW + 96, KP), 1), 1.0, 0.0).astype(BF16)
    for q in range(CHUNKS):
        kept[RP * q + 16 : RP * q + RP, :] = jnp.zeros((16, CHUNK), BF16)
    lane = iota((8, CHUNK), 1)
    mod = mod_o(lane)
    over = (lane - mod) // O
    group = iota((8, 128), 0) // 4
    for copy in copies[:3]:
        copy.wait()
    here = place()
    a, first = here // 4, ROWS * (here % 4)
    row = a_irrep[0, a] ^ to_rows(occ[...].astype(F32), RP, first).astype(I32)
    occ_t = lookup(padded(occ[...]), mod)
    want[...] = (row ^ occ_t[:1]).astype(BF16)
    for half in range(2):
        lanes = [jnp.broadcast_to(c_lanes[:, 128 * v : 128 * v + 128], (8, 128)) for v in (2 * half, 2 * half + 1)]
        source = jnp.where(group == 0, lanes[0], lanes[1])
        have[8 * half : 8 * half + 8, :] = lookup(source, 32 * (iota((8, CHUNK), 0) % 4) + over).astype(F32)
    for x in range(XS):
        if x == XS // 2:
            rest.wait()
        source, skip = (early, 0) if x < XS // 2 else (late, EARLY)
        part = slice(RP * PER_X * x, RP * PER_X * (x + 1))
        for q in range(PER_X * x, PER_X * (x + 1)):
            mask = want[:ROWS, :] == have[q : q + 1, :].astype(BF16)
            got = source[:, CHUNK * q - skip : CHUNK * (q + 1) - skip]
            kept[RP * q : RP * q + ROWS, :] = jnp.where(mask, got, jnp.zeros((), BF16))
        for j in range(4):
            full = jnp.dot(
                kept[part, 768 * j : 768 * j + WINDOW],
                pick[96 - 32 * j : 96 - 32 * j + WINDOW, :],
                preferred_element_type=F32,
            )
            for h in range(PER_X):
                lanes = slice(KP * (4 * h + j), KP * (4 * h + j + 1))
                packed[x, :, lanes] = full[RP * h : RP * (h + 1)].astype(BF16)
        for y in range(YS):
            send(x, y).start()
    for copy in copies[3:]:
        copy.wait()
    wide = 4 * NP
    col = (by_slab(b_irrep, I32) ^ occ_t[:, :wide])[:1, :COLS]
    column_energy = (by_slab(eps_b, F32) - lookup(padded(eps_occ[...]), mod[:, :wide]))[:1, :COLS]
    energy[...] = (eps_a[0, a] - to_rows(eps_occ[...], ROWS, first)) + column_energy
    same[...] = jnp.where(row[:ROWS] == col, 1.0, 0.0)
    for x in range(XS):
        for y in range(YS):
            send(x, y).wait()


def mm_kernel(t_ref, w_ref, out_ref):
    w_t = jnp.concatenate([w_ref[z] for z in range(ZS)], axis=1)
    out_ref[...] = lax.dot_general(
        t_ref[...], w_t, (((1,), (1,)), ((), ())), preferred_element_type=F32
    )


def end_kernel(energy_ref, same_ref, part_ref, out_ref):
    for n in range(4):
        lo, hi = NP * n, min(NP * n + NP, COLS)
        total = part_ref[n, :ROWS, : hi - lo]
        for x in range(1, XS):
            total = total + part_ref[YS * x + n, :ROWS, : hi - lo]
        total = jnp.where(same_ref[:, lo:hi] > 0.5, total, 0.0)
        out_ref[:, lo:hi] = total / energy_ref[:, lo:hi]


def call(kernel, out, flops, moved, room, **rest):
    return pl.pallas_call(
        kernel,
        out_shape=out,
        cost_estimate=pl.CostEstimate(flops=flops, bytes_accessed=moved, transcendentals=0),
        compiler_params=pltpu.CompilerParams(vmem_limit_bytes=room * 2**20),
        **rest,
    )


def per_device(t_slab, w_cycle, a_irrep, b_irrep, c_irrep, occ_irrep, eps_a, eps_b, eps_occ):
    vmem, smem, dma = pltpu.VMEM, pltpu.SMEM, pltpu.SemaphoreType.DMA
    struct = jax.ShapeDtypeStruct
    whole = pl.BlockSpec(memory_space=pltpu.VMEM)
    lanes = lambda vector: vector.reshape(1, -1)
    a_row, b_row, c_row, occ, eo = (lanes(v) for v in (a_irrep, b_irrep, c_irrep, occ_irrep, eps_occ))
    w_parts, t_near = call(
        head_kernel,
        [pltpu.HBM((4 * NP, KP), BF16), vmem((ROWS, EARLY), BF16)],
        10**7, 10**6, 56,
        in_specs=[HBM] * 5,
        out_specs=[HBM, whole],
        scratch_shapes=[
            smem((1, 4), I32), smem((1, 512), I32), vmem((1, O), I32), vmem((COLS, O), BF16),
            vmem((4 * NP, KP), BF16), dma((4,)), dma, dma,
        ],
    )(b_row, c_row, occ, w_cycle.T, t_slab)
    w_got = lax.all_to_all(w_parts.reshape(8, NP // 2, KP), "rep", split_axis=0, concat_axis=0, tiled=True)
    w_own = jnp.sum(w_got, axis=0, dtype=BF16)
    t_parts, energy, same = call(
        t_kernel,
        [pltpu.HBM((XS * YS, RP, ZS * KP), BF16), vmem((ROWS, COLS), F32), vmem((ROWS, COLS), F32)],
        4 * 10**9, 4 * 10**6, 55,
        in_specs=[HBM] * 7 + [whole, HBM],
        out_specs=[HBM, whole, whole],
        scratch_shapes=[
            smem((1, 128), I32), vmem((1, 512), I32), vmem((1, O), I32), smem((1, 4), I32), smem((1, 128), F32),
            smem((1, 4), F32), vmem((1, O), F32), vmem((ROWS, EARLY), BF16), vmem((RP, CHUNK), BF16), vmem((CHUNKS, CHUNK), F32),
            vmem((WINDOW + 96, KP), BF16), vmem((CHUNKS * RP, CHUNK), BF16), vmem((XS, RP, ZS * KP), BF16),
            dma((7,)), dma, dma((XS * YS,)),
        ],
    )(
        a_row, c_row, occ, b_row, lanes(eps_a), lanes(eps_b), eo,
        pltpu.with_memory_space_constraint(t_near, pltpu.VMEM), t_slab,
    )
    t_got = lax.all_to_all(
        t_parts, ("idx", "rep"), split_axis=0, concat_axis=0, axis_index_groups=CORE_PLANES, tiled=True
    )
    w_own, t_parts = lax.optimization_barrier((w_own, t_parts))
    w_z = lax.all_gather(w_own, ("idx", "rep"), axis=0, axis_index_groups=Z_CORE_GROUPS)
    partial = call(
        mm_kernel, struct((XS * YS * RP, NP), F32), 2 * 512 * 2048 * 128, 3 * 10**6, 24,
        in_specs=[whole] * 2, out_specs=whole,
    )(t_got.reshape(-1, ZS * KP), w_z.reshape(ZS, NP, KP))
    ends = lax.all_to_all(
        partial.reshape(-1, RP, NP), ("idx", "rep"), split_axis=0, concat_axis=0,
        axis_index_groups=CORE_PLANES, tiled=True,
    )
    return call(
        end_kernel, struct((ROWS, COLS), F32), 10**6, 10**6, 24, in_specs=[whole] * 3, out_specs=whole
    )(*(pltpu.with_memory_space_constraint(near, pltpu.VMEM) for near in (energy, same)), ends)


def solution(mesh):
    in_specs = (P(("idx", "rep"), None), P(("idx", "rep"), None), P(), P(), P(), P(), P(), P(), P())
    out_specs = P(("idx", "rep"), None)
    return jax.shard_map(
        per_device, mesh=mesh, in_specs=in_specs, out_specs=out_specs, check_vma=False
    )
```

```python
import jax
import jax.numpy as jnp
from jax import lax
from jax.experimental import pallas as pl
from jax.experimental.pallas import tpu as pltpu
from jax.sharding import PartitionSpec as P

O = 100
G = 8
COLS = 400
SLABS = 4
SP = 112
NP = 128
KP = 128
RP = 32
ROWS = 25
GROUP = G * O
CHUNK = 4 * GROUP
CHUNKS = 16
PER_X = 4
EARLY = CHUNKS // 2 * CHUNK
WINDOW = 896
F32, BF16, I32 = jnp.float32, jnp.bfloat16, jnp.int32
HBM = pl.BlockSpec(memory_space=pltpu.HBM)
ZS, XS, YS, CS = 16, 4, 4, 2
Z_GROUPS = [[x * ZS + z for z in range(ZS)] for x in range(XS)]
WORK_GROUPS = [
    [(x * ZS + z) * YS * CS + (2 * high + low) * CS + c for x in range(XS) for low in range(2)]
    for z in range(ZS)
    for high in range(2)
    for c in range(CS)
]
Z_CORE_GROUPS = [
    [(x * ZS + z) * YS * CS + y * CS + c for z in range(ZS) for c in range(CS)]
    for x in range(XS)
    for y in range(YS)
]


def iota(shape, dim):
    return lax.broadcasted_iota(I32, shape, dim)


def mod_o(n):
    return n - O * jnp.floor((n.astype(F32) + 0.5) * (1.0 / O)).astype(I32)


def to_rows(lanes, count, first):
    shape = (count, lanes.shape[1])
    hit = iota(shape, 1) == iota(shape, 0) + first
    return jnp.sum(jnp.where(hit, lanes, 0.0), axis=1, keepdims=True)


def lookup(lanes, index):
    parts = [
        jnp.take_along_axis(lanes, index[:, at : at + 128], axis=1) for at in range(0, index.shape[1], 128)
    ]
    return jnp.concatenate(parts, axis=1)


def fetch(sources, targets, sems):
    copies = [pltpu.make_async_copy(s, t, sems.at[i]) for i, (s, t) in enumerate(zip(sources, targets))]
    for copy in copies:
        copy.start()
    return copies


def place():
    return lax.axis_index("idx") * (YS * CS) + lax.axis_index("rep")


def padded(lanes):
    wide = jnp.concatenate([lanes, jnp.zeros((1, 128 - O), lanes.dtype)], axis=1)
    return jnp.broadcast_to(wide, (8, 128))


def head_kernel(
    b_hbm, c_hbm, occ_hbm, w_hbm, t_hbm, out_hbm, t_ref, b_irrep, c_irrep, occ, w_ref, out_ref, sems, t_sem, out_sem
):
    copies = fetch((b_hbm, c_hbm, occ_hbm, w_hbm), (b_irrep, c_irrep, occ, w_ref), sems)
    early = pltpu.make_async_copy(t_hbm.at[:, pl.ds(0, EARLY)], t_ref, t_sem)
    early.start()
    out_ref[...] = jnp.zeros_like(out_ref)
    for copy in copies:
        copy.wait()
    column = to_rows(occ[...].astype(F32), O, 0).astype(I32)
    row = c_irrep[0, place()] ^ occ[...]
    same = column ^ row
    w = w_ref[...].astype(F32)
    for b in range(SLABS):
        kept = jnp.where(same == b_irrep[0, b], w[O * b : O * (b + 1)], 0.0).astype(BF16)
        for high in range(2):
            out_ref[SLABS * high + b, :O, :O] = kept
    send = pltpu.make_async_copy(out_ref, out_hbm, out_sem)
    send.start()
    send.wait()
    early.wait()


def t_kernel(
    a_hbm, c_hbm, occ_hbm, b_hbm, ea_hbm, eb_hbm, eo_hbm, early, t_hbm, out_hbm, energy, same,
    a_irrep, c_lanes, occ, b_irrep, eps_a, eps_b, eps_occ, late, want, have, pick, kept, packed, sems, t_sem, o_sems,
):
    def send(x, y):
        return pltpu.make_async_copy(packed.at[x], out_hbm.at[2 * x + y], o_sems.at[2 * x + y])

    copies = fetch(
        (a_hbm, c_hbm, occ_hbm, b_hbm, ea_hbm, eb_hbm, eo_hbm),
        (a_irrep, c_lanes, occ, b_irrep, eps_a, eps_b, eps_occ),
        sems,
    )
    rest = pltpu.make_async_copy(t_hbm.at[:, pl.ds(EARLY, EARLY)], late, t_sem)
    rest.start()
    at = iota((WINDOW + 96, 1), 0) - 96
    k = jnp.where((at >= 0) & (at < GROUP), mod_o(jnp.maximum(at, 0)), -1)
    pick[...] = jnp.where(k == iota((WINDOW + 96, KP), 1), 1.0, 0.0).astype(BF16)
    for q in range(CHUNKS):
        kept[RP * q + 16 : RP * q + RP, :] = jnp.zeros((16, CHUNK), BF16)
    lane = iota((8, CHUNK), 1)
    mod = mod_o(lane)
    over = (lane - mod) // O
    group = iota((8, 128), 0) // 4
    for copy in copies[:3]:
        copy.wait()
    here = place()
    a, first = here // 4, ROWS * (here % 4)
    row = a_irrep[0, a] ^ to_rows(occ[...].astype(F32), RP, first).astype(I32)
    occ_t = lookup(padded(occ[...]), mod)
    want[...] = (row ^ occ_t[:1]).astype(BF16)
    for half in range(2):
        lanes = [jnp.broadcast_to(c_lanes[:, 128 * v : 128 * v + 128], (8, 128)) for v in (2 * half, 2 * half + 1)]
        source = jnp.where(group == 0, lanes[0], lanes[1])
        have[8 * half : 8 * half + 8, :] = lookup(source, 32 * (iota((8, CHUNK), 0) % 4) + over).astype(F32)
    for x in range(XS):
        if x == XS // 2:
            rest.wait()
        source, skip = (early, 0) if x < XS // 2 else (late, EARLY)
        part = slice(RP * PER_X * x, RP * PER_X * (x + 1))
        for q in range(PER_X * x, PER_X * (x + 1)):
            mask = want[:ROWS, :] == have[q : q + 1, :].astype(BF16)
            got = source[:, CHUNK * q - skip : CHUNK * (q + 1) - skip]
            kept[RP * q : RP * q + ROWS, :] = jnp.where(mask, got, jnp.zeros((), BF16))
        for j in range(4):
            full = jnp.dot(
                kept[part, 768 * j : 768 * j + WINDOW],
                pick[96 - 32 * j : 96 - 32 * j + WINDOW, :],
                preferred_element_type=F32,
            )
            for h in range(PER_X):
                lanes = slice(KP * (4 * h + j), KP * (4 * h + j + 1))
                packed[x, :, lanes] = full[RP * h : RP * (h + 1)].astype(BF16)
        for y in range(2):
            send(x, y).start()
    for copy in copies[3:]:
        copy.wait()
    row_energy = eps_a[0, a] - to_rows(eps_occ[...], ROWS, first)
    for b in range(SLABS):
        energy[b] = row_energy + (eps_b[0, b] - eps_occ[...])
        same[b] = jnp.where(row[:ROWS] == (b_irrep[0, b] ^ occ[...]), 1.0, 0.0)
    for x in range(XS):
        for y in range(2):
            send(x, y).wait()


def mm_kernel(t_ref, w_ref, out_ref):
    out_ref[...] = jnp.zeros_like(out_ref)
    for c in range(CS):
        w_t = jnp.concatenate([w_ref[CS * z + c] for z in range(ZS)], axis=1)
        got = lax.dot_general(t_ref[...], w_t, (((1,), (1,)), ((), ())), preferred_element_type=F32)
        out_ref[:, NP * c : NP * c + SP] = got


def end_kernel(energy_ref, same_ref, part_ref, out_ref):
    for b in range(SLABS):
        low, c = divmod(b, CS)
        lanes = slice(NP * c, NP * c + O)
        total = part_ref[low, :ROWS, lanes]
        for x in range(1, XS):
            total = total + part_ref[2 * x + low, :ROWS, lanes]
        total = jnp.where(same_ref[b] > 0.5, total, 0.0)
        out_ref[:, O * b : O * (b + 1)] = total / energy_ref[b]


def call(kernel, out, flops, moved, room, **rest):
    return pl.pallas_call(
        kernel,
        out_shape=out,
        cost_estimate=pl.CostEstimate(flops=flops, bytes_accessed=moved, transcendentals=0),
        compiler_params=pltpu.CompilerParams(vmem_limit_bytes=room * 2**20),
        **rest,
    )


def per_device(t_slab, w_cycle, a_irrep, b_irrep, c_irrep, occ_irrep, eps_a, eps_b, eps_occ):
    vmem, smem, dma = pltpu.VMEM, pltpu.SMEM, pltpu.SemaphoreType.DMA
    struct = jax.ShapeDtypeStruct
    whole = pl.BlockSpec(memory_space=pltpu.VMEM)
    lanes = lambda vector: vector.reshape(1, -1)
    a_row, b_row, c_row, occ, eo = (lanes(v) for v in (a_irrep, b_irrep, c_irrep, occ_irrep, eps_occ))
    w_parts, t_near = call(
        head_kernel,
        [pltpu.HBM((2 * SLABS, SP, KP), BF16), vmem((ROWS, EARLY), BF16)],
        10**7, 10**6, 56,
        in_specs=[HBM] * 5,
        out_specs=[HBM, whole],
        scratch_shapes=[
            smem((1, 4), I32), smem((1, 512), I32), vmem((1, O), I32), vmem((COLS, O), BF16),
            vmem((2 * SLABS, SP, KP), BF16), dma((4,)), dma, dma,
        ],
    )(b_row, c_row, occ, w_cycle.T, t_slab)
    w_got = lax.all_to_all(w_parts, "rep", split_axis=0, concat_axis=0, tiled=True)
    w_own = jnp.sum(w_got, axis=0, dtype=BF16)
    t_parts, energy, same = call(
        t_kernel,
        [pltpu.HBM((2 * XS, RP, ZS * KP), BF16), vmem((SLABS, ROWS, O), F32), vmem((SLABS, ROWS, O), F32)],
        4 * 10**9, 4 * 10**6, 55,
        in_specs=[HBM] * 7 + [whole, HBM],
        out_specs=[HBM, whole, whole],
        scratch_shapes=[
            smem((1, 128), I32), vmem((1, 512), I32), vmem((1, O), I32), smem((1, 4), I32), smem((1, 128), F32),
            smem((1, 4), F32), vmem((1, O), F32), vmem((ROWS, EARLY), BF16), vmem((RP, CHUNK), BF16), vmem((CHUNKS, CHUNK), F32),
            vmem((WINDOW + 96, KP), BF16), vmem((CHUNKS * RP, CHUNK), BF16), vmem((XS, RP, ZS * KP), BF16),
            dma((7,)), dma, dma((2 * XS,)),
        ],
    )(
        a_row, c_row, occ, b_row, lanes(eps_a), lanes(eps_b), eo,
        pltpu.with_memory_space_constraint(t_near, pltpu.VMEM), t_slab,
    )
    t_got = lax.all_to_all(
        t_parts, ("idx", "rep"), split_axis=0, concat_axis=0, axis_index_groups=WORK_GROUPS, tiled=True
    )
    w_own, t_parts = lax.optimization_barrier((w_own, t_parts))
    w_z = lax.all_gather(w_own, ("idx", "rep"), axis=0, axis_index_groups=Z_CORE_GROUPS)
    partial = call(
        mm_kernel, struct((2 * XS * RP, CS * NP), F32), 2 * 512 * 2048 * 128, 3 * 10**6, 24,
        in_specs=[whole] * 2, out_specs=whole,
    )(t_got.reshape(-1, ZS * KP), w_z)
    ends = lax.all_to_all(
        partial.reshape(2 * XS, RP, CS * NP), ("idx", "rep"), split_axis=0, concat_axis=0,
        axis_index_groups=WORK_GROUPS, tiled=True,
    )
    return call(
        end_kernel, struct((ROWS, COLS), F32), 10**6, 10**6, 24, in_specs=[whole] * 3, out_specs=whole
    )(*(pltpu.with_memory_space_constraint(near, pltpu.VMEM) for near in (energy, same)), ends)


def solution(mesh):
    in_specs = (P(("idx", "rep"), None), P(("idx", "rep"), None), P(), P(), P(), P(), P(), P(), P())
    out_specs = P(("idx", "rep"), None)
    return jax.shard_map(
        per_device, mesh=mesh, in_specs=in_specs, out_specs=out_specs, check_vma=False
    )
```

```python
import jax
import jax.numpy as jnp
from jax import lax
from jax.experimental import pallas as pl
from jax.experimental.pallas import tpu as pltpu
from jax.sharding import PartitionSpec as P

O = 100
G = 8
COLS = 400
SLABS = 4
SP = 112
NP = 128
KP = 128
RP = 32
ROWS = 25
GROUP = G * O
CHUNK = 4 * GROUP
CHUNKS = 16
PER_X = 4
EARLY = CHUNKS // 2 * CHUNK
WINDOW = 896
F32, BF16, I32 = jnp.float32, jnp.bfloat16, jnp.int32
HBM = pl.BlockSpec(memory_space=pltpu.HBM)
ZS, XS, YS, CS = 16, 4, 4, 2
Z_GROUPS = [[x * ZS + z for z in range(ZS)] for x in range(XS)]
WORK_GROUPS = [
    [(x * ZS + z) * YS * CS + (2 * high + low) * CS + c for x in range(XS) for low in range(2)]
    for z in range(ZS)
    for high in range(2)
    for c in range(CS)
]
Z_CORE_GROUPS = [
    [(x * ZS + z) * YS * CS + y * CS + c for z in range(ZS) for c in range(CS)]
    for x in range(XS)
    for y in range(YS)
]


def iota(shape, dim):
    return lax.broadcasted_iota(I32, shape, dim)


def mod_o(n):
    return n - O * jnp.floor((n.astype(F32) + 0.5) * (1.0 / O)).astype(I32)


def to_rows(lanes, count, first):
    shape = (count, lanes.shape[1])
    hit = iota(shape, 1) == iota(shape, 0) + first
    return jnp.sum(jnp.where(hit, lanes, 0.0), axis=1, keepdims=True)


def lookup(lanes, index):
    parts = [
        jnp.take_along_axis(lanes, index[:, at : at + 128], axis=1) for at in range(0, index.shape[1], 128)
    ]
    return jnp.concatenate(parts, axis=1)


def fetch(sources, targets, sems):
    copies = [pltpu.make_async_copy(s, t, sems.at[i]) for i, (s, t) in enumerate(zip(sources, targets))]
    for copy in copies:
        copy.start()
    return copies


def place():
    return lax.axis_index("idx") * (YS * CS) + lax.axis_index("rep")


def padded(lanes):
    wide = jnp.concatenate([lanes, jnp.zeros((1, 128 - O), lanes.dtype)], axis=1)
    return jnp.broadcast_to(wide, (8, 128))


def head_kernel(
    b_hbm, c_hbm, occ_hbm, w_hbm, t_hbm, out_hbm, t_ref, b_irrep, c_irrep, occ, w_ref, out_ref, sems, t_sem, out_sem
):
    copies = fetch((b_hbm, c_hbm, occ_hbm, w_hbm), (b_irrep, c_irrep, occ, w_ref), sems)
    early = pltpu.make_async_copy(t_hbm.at[:, pl.ds(0, EARLY)], t_ref, t_sem)
    early.start()
    out_ref[...] = jnp.zeros_like(out_ref)
    for copy in copies:
        copy.wait()
    column = to_rows(occ[...].astype(F32), O, 0).astype(I32)
    row = c_irrep[0, place()] ^ occ[...]
    same = column ^ row
    w = w_ref[...].astype(F32)
    for b in range(SLABS):
        kept = jnp.where(same == b_irrep[0, b], w[O * b : O * (b + 1)], 0.0).astype(BF16)
        out_ref[b, :O, :O] = kept
    sends = [
        pltpu.make_async_copy(out_ref, out_hbm.at[pl.ds(SLABS * high, SLABS)], out_sem.at[high])
        for high in range(2)
    ]
    for send in sends:
        send.start()
    for send in sends:
        send.wait()
    early.wait()


def t_kernel(
    a_hbm, c_hbm, occ_hbm, b_hbm, ea_hbm, eb_hbm, eo_hbm, early, t_hbm, out_hbm, energy, same,
    a_irrep, c_lanes, occ, b_irrep, eps_a, eps_b, eps_occ, late, want, have, pick, kept, packed, sems, t_sem, o_sems,
):
    def send(x, y):
        return pltpu.make_async_copy(packed.at[x], out_hbm.at[2 * x + y], o_sems.at[2 * x + y])

    copies = fetch(
        (a_hbm, c_hbm, occ_hbm, b_hbm, ea_hbm, eb_hbm, eo_hbm),
        (a_irrep, c_lanes, occ, b_irrep, eps_a, eps_b, eps_occ),
        sems,
    )
    rest = pltpu.make_async_copy(t_hbm.at[:, pl.ds(EARLY, EARLY)], late, t_sem)
    rest.start()
    at = iota((WINDOW + 96, 1), 0) - 96
    k = jnp.where((at >= 0) & (at < GROUP), mod_o(jnp.maximum(at, 0)), -1)
    pick[...] = jnp.where(k == iota((WINDOW + 96, KP), 1), 1.0, 0.0).astype(BF16)
    for q in range(CHUNKS):
        kept[RP * q + 16 : RP * q + RP, :] = jnp.zeros((16, CHUNK), BF16)
    lane = iota((8, CHUNK), 1)
    mod = mod_o(lane)
    over = (lane - mod) // O
    group = iota((8, 128), 0) // 4
    for copy in copies[:3]:
        copy.wait()
    here = place()
    a, first = here // 4, ROWS * (here % 4)
    row = a_irrep[0, a] ^ to_rows(occ[...].astype(F32), RP, first).astype(I32)
    occ_t = lookup(padded(occ[...]), mod)
    want[...] = (row ^ occ_t[:1]).astype(BF16)
    for half in range(2):
        lanes = [jnp.broadcast_to(c_lanes[:, 128 * v : 128 * v + 128], (8, 128)) for v in (2 * half, 2 * half + 1)]
        source = jnp.where(group == 0, lanes[0], lanes[1])
        have[8 * half : 8 * half + 8, :] = lookup(source, 32 * (iota((8, CHUNK), 0) % 4) + over).astype(F32)
    for x in range(XS):
        if x == XS // 2:
            rest.wait()
        source, skip = (early, 0) if x < XS // 2 else (late, EARLY)
        part = slice(RP * PER_X * x, RP * PER_X * (x + 1))
        for q in range(PER_X * x, PER_X * (x + 1)):
            mask = want[:ROWS, :] == have[q : q + 1, :].astype(BF16)
            got = source[:, CHUNK * q - skip : CHUNK * (q + 1) - skip]
            kept[RP * q : RP * q + ROWS, :] = jnp.where(mask, got, jnp.zeros((), BF16))
        for j in range(4):
            full = jnp.dot(
                kept[part, 768 * j : 768 * j + WINDOW],
                pick[96 - 32 * j : 96 - 32 * j + WINDOW, :],
                preferred_element_type=F32,
            )
            for h in range(PER_X):
                lanes = slice(KP * (4 * h + j), KP * (4 * h + j + 1))
                packed[x, :, lanes] = full[RP * h : RP * (h + 1)].astype(BF16)
        for y in range(2):
            send(x, y).start()
    for copy in copies[3:]:
        copy.wait()
    row_energy = eps_a[0, a] - to_rows(eps_occ[...], ROWS, first)
    for b in range(SLABS):
        energy[b] = row_energy + (eps_b[0, b] - eps_occ[...])
        same[b] = jnp.where(row[:ROWS] == (b_irrep[0, b] ^ occ[...]), 1.0, 0.0)
    for x in range(XS):
        for y in range(2):
            send(x, y).wait()


def mm_kernel(t_ref, w_ref, out_ref):
    none = jnp.zeros((NP - SP, ZS * KP), BF16)
    rows = []
    for c in range(CS):
        rows += [jnp.concatenate([w_ref[CS * z + c] for z in range(ZS)], axis=1), none]
    w_t = jnp.concatenate(rows, axis=0)
    out_ref[...] = lax.dot_general(
        t_ref[...], w_t, (((1,), (1,)), ((), ())), preferred_element_type=F32
    )


def end_kernel(energy_ref, same_ref, part_ref, out_ref):
    for b in range(SLABS):
        low, c = divmod(b, CS)
        lanes = slice(NP * c, NP * c + O)
        total = part_ref[low, :ROWS, lanes]
        for x in range(1, XS):
            total = total + part_ref[2 * x + low, :ROWS, lanes]
        total = jnp.where(same_ref[b] > 0.5, total, 0.0)
        out_ref[:, O * b : O * (b + 1)] = total / energy_ref[b]


def call(kernel, out, flops, moved, room, **rest):
    return pl.pallas_call(
        kernel,
        out_shape=out,
        cost_estimate=pl.CostEstimate(flops=flops, bytes_accessed=moved, transcendentals=0),
        compiler_params=pltpu.CompilerParams(vmem_limit_bytes=room * 2**20),
        **rest,
    )


def per_device(t_slab, w_cycle, a_irrep, b_irrep, c_irrep, occ_irrep, eps_a, eps_b, eps_occ):
    vmem, smem, dma = pltpu.VMEM, pltpu.SMEM, pltpu.SemaphoreType.DMA
    struct = jax.ShapeDtypeStruct
    whole = pl.BlockSpec(memory_space=pltpu.VMEM)
    lanes = lambda vector: vector.reshape(1, -1)
    a_row, b_row, c_row, occ, eo = (lanes(v) for v in (a_irrep, b_irrep, c_irrep, occ_irrep, eps_occ))
    w_parts, t_near = call(
        head_kernel,
        [pltpu.HBM((2 * SLABS, SP, KP), BF16), vmem((ROWS, EARLY), BF16)],
        10**7, 10**6, 56,
        in_specs=[HBM] * 5,
        out_specs=[HBM, whole],
        scratch_shapes=[
            smem((1, 4), I32), smem((1, 512), I32), vmem((1, O), I32), vmem((COLS, O), BF16),
            vmem((SLABS, SP, KP), BF16), dma((4,)), dma, dma((2,)),
        ],
    )(b_row, c_row, occ, w_cycle.T, t_slab)
    w_got = lax.all_to_all(w_parts, "rep", split_axis=0, concat_axis=0, tiled=True)
    w_own = jnp.sum(w_got, axis=0, dtype=BF16)
    t_parts, energy, same = call(
        t_kernel,
        [pltpu.HBM((2 * XS, RP, ZS * KP), BF16), vmem((SLABS, ROWS, O), F32), vmem((SLABS, ROWS, O), F32)],
        4 * 10**9, 4 * 10**6, 55,
        in_specs=[HBM] * 7 + [whole, HBM],
        out_specs=[HBM, whole, whole],
        scratch_shapes=[
            smem((1, 128), I32), vmem((1, 512), I32), vmem((1, O), I32), smem((1, 4), I32), smem((1, 128), F32),
            smem((1, 4), F32), vmem((1, O), F32), vmem((ROWS, EARLY), BF16), vmem((RP, CHUNK), BF16), vmem((CHUNKS, CHUNK), F32),
            vmem((WINDOW + 96, KP), BF16), vmem((CHUNKS * RP, CHUNK), BF16), vmem((XS, RP, ZS * KP), BF16),
            dma((7,)), dma, dma((2 * XS,)),
        ],
    )(
        a_row, c_row, occ, b_row, lanes(eps_a), lanes(eps_b), eo,
        pltpu.with_memory_space_constraint(t_near, pltpu.VMEM), t_slab,
    )
    t_got = lax.all_to_all(
        t_parts, ("idx", "rep"), split_axis=0, concat_axis=0, axis_index_groups=WORK_GROUPS, tiled=True
    )
    w_own, t_parts = lax.optimization_barrier((w_own, t_parts))
    w_z = lax.all_gather(w_own, ("idx", "rep"), axis=0, axis_index_groups=Z_CORE_GROUPS)
    partial = call(
        mm_kernel, struct((2 * XS * RP, CS * NP), F32), 2 * 512 * 2048 * 128, 3 * 10**6, 24,
        in_specs=[whole] * 2, out_specs=whole,
    )(t_got.reshape(-1, ZS * KP), w_z)
    ends = lax.all_to_all(
        partial.reshape(2 * XS, RP, CS * NP), ("idx", "rep"), split_axis=0, concat_axis=0,
        axis_index_groups=WORK_GROUPS, tiled=True,
    )
    return call(
        end_kernel, struct((ROWS, COLS), F32), 10**6, 10**6, 24, in_specs=[whole] * 3, out_specs=whole
    )(*(pltpu.with_memory_space_constraint(near, pltpu.VMEM) for near in (energy, same)), ends)


def solution(mesh):
    in_specs = (P(("idx", "rep"), None), P(("idx", "rep"), None), P(), P(), P(), P(), P(), P(), P())
    out_specs = P(("idx", "rep"), None)
    return jax.shard_map(
        per_device, mesh=mesh, in_specs=in_specs, out_specs=out_specs, check_vma=False
    )
```

```python
import jax
import jax.numpy as jnp
from jax import lax
from jax.experimental import pallas as pl
from jax.experimental.pallas import tpu as pltpu
from jax.sharding import PartitionSpec as P

O = 100
G = 8
COLS = 400
SLABS = 4
SP = 112
NP = 128
KP = 128
RP = 32
ROWS = 25
GROUP = G * O
CHUNK = 4 * GROUP
CHUNKS = 16
PER_X = 4
EARLY = CHUNKS // 2 * CHUNK
WINDOW = 896
F32, BF16, I32 = jnp.float32, jnp.bfloat16, jnp.int32
HBM = pl.BlockSpec(memory_space=pltpu.HBM)
ZS, XS, YS, CS = 16, 4, 4, 2
Z_GROUPS = [[x * ZS + z for z in range(ZS)] for x in range(XS)]
WORK_GROUPS = [
    [(x * ZS + z) * YS * CS + (2 * high + low) * CS + c for x in range(XS) for low in range(2)]
    for z in range(ZS)
    for high in range(2)
    for c in range(CS)
]
Z_CORE_GROUPS = [
    [(x * ZS + z) * YS * CS + y * CS + c for z in range(ZS) for c in range(CS)]
    for x in range(XS)
    for y in range(YS)
]


def iota(shape, dim):
    return lax.broadcasted_iota(I32, shape, dim)


def mod_o(n):
    return n - O * jnp.floor((n.astype(F32) + 0.5) * (1.0 / O)).astype(I32)


def to_rows(lanes, count, first):
    shape = (count, lanes.shape[1])
    hit = iota(shape, 1) == iota(shape, 0) + first
    return jnp.sum(jnp.where(hit, lanes, 0.0), axis=1, keepdims=True)


def lookup(lanes, index):
    parts = [
        jnp.take_along_axis(lanes, index[:, at : at + 128], axis=1) for at in range(0, index.shape[1], 128)
    ]
    return jnp.concatenate(parts, axis=1)


def fetch(sources, targets, sems):
    copies = [pltpu.make_async_copy(s, t, sems.at[i]) for i, (s, t) in enumerate(zip(sources, targets))]
    for copy in copies:
        copy.start()
    return copies


def place():
    return lax.axis_index("idx") * (YS * CS) + lax.axis_index("rep")


def padded(lanes):
    wide = jnp.concatenate([lanes, jnp.zeros((1, 128 - O), lanes.dtype)], axis=1)
    return jnp.broadcast_to(wide, (8, 128))


def head_kernel(
    b_hbm, c_hbm, occ_hbm, w_hbm, t_hbm, out_hbm, t_ref, b_irrep, c_irrep, occ, w_ref, out_ref, sems, t_sem, out_sem
):
    copies = fetch((b_hbm, c_hbm, occ_hbm, w_hbm), (b_irrep, c_irrep, occ, w_ref), sems)
    early = pltpu.make_async_copy(t_hbm.at[:, pl.ds(0, EARLY)], t_ref, t_sem)
    early.start()
    out_ref[...] = jnp.zeros_like(out_ref)
    for copy in copies[:3]:
        copy.wait()
    column = to_rows(occ[...].astype(F32), O, 0).astype(I32)
    same = column ^ (c_irrep[0, place()] ^ occ[...])
    kept = [same == b_irrep[0, b] for b in range(SLABS)]
    copies[3].wait()
    w = w_ref[...].astype(F32)
    sends = []
    for b in range(SLABS):
        out_ref[b, :O, :O] = jnp.where(kept[b], w[O * b : O * (b + 1)], 0.0).astype(BF16)
        for high in range(2):
            at = SLABS * high + b
            sends.append(pltpu.make_async_copy(out_ref.at[b], out_hbm.at[at], out_sem.at[at]))
            sends[-1].start()
    for send in sends:
        send.wait()
    early.wait()


def t_kernel(
    a_hbm, c_hbm, occ_hbm, b_hbm, ea_hbm, eb_hbm, eo_hbm, early, t_hbm, out_hbm, energy, same,
    a_irrep, c_lanes, occ, b_irrep, eps_a, eps_b, eps_occ, late, want, have, pick, kept, packed, sems, t_sem, o_sems,
):
    def send(x, y):
        return pltpu.make_async_copy(packed.at[x], out_hbm.at[2 * x + y], o_sems.at[2 * x + y])

    copies = fetch(
        (a_hbm, c_hbm, occ_hbm, b_hbm, ea_hbm, eb_hbm, eo_hbm),
        (a_irrep, c_lanes, occ, b_irrep, eps_a, eps_b, eps_occ),
        sems,
    )
    rest = pltpu.make_async_copy(t_hbm.at[:, pl.ds(EARLY, EARLY)], late, t_sem)
    rest.start()
    at = iota((WINDOW + 96, 1), 0) - 96
    k = jnp.where((at >= 0) & (at < GROUP), mod_o(jnp.maximum(at, 0)), -1)
    pick[...] = jnp.where(k == iota((WINDOW + 96, KP), 1), 1.0, 0.0).astype(BF16)
    for q in range(CHUNKS):
        kept[RP * q + 16 : RP * q + RP, :] = jnp.zeros((16, CHUNK), BF16)
    lane = iota((8, CHUNK), 1)
    mod = mod_o(lane)
    over = (lane - mod) // O
    group = iota((8, 128), 0) // 4
    for copy in copies[:3]:
        copy.wait()
    here = place()
    a, first = here // 4, ROWS * (here % 4)
    row = a_irrep[0, a] ^ to_rows(occ[...].astype(F32), RP, first).astype(I32)
    occ_t = lookup(padded(occ[...]), mod)
    want[...] = (row ^ occ_t[:1]).astype(BF16)
    for half in range(2):
        lanes = [jnp.broadcast_to(c_lanes[:, 128 * v : 128 * v + 128], (8, 128)) for v in (2 * half, 2 * half + 1)]
        source = jnp.where(group == 0, lanes[0], lanes[1])
        have[8 * half : 8 * half + 8, :] = lookup(source, 32 * (iota((8, CHUNK), 0) % 4) + over).astype(F32)
    for x in range(XS):
        if x == XS // 2:
            rest.wait()
        source, skip = (early, 0) if x < XS // 2 else (late, EARLY)
        part = slice(RP * PER_X * x, RP * PER_X * (x + 1))
        for q in range(PER_X * x, PER_X * (x + 1)):
            mask = want[:ROWS, :] == have[q : q + 1, :].astype(BF16)
            got = source[:, CHUNK * q - skip : CHUNK * (q + 1) - skip]
            kept[RP * q : RP * q + ROWS, :] = jnp.where(mask, got, jnp.zeros((), BF16))
        for j in range(4):
            full = jnp.dot(
                kept[part, 768 * j : 768 * j + WINDOW],
                pick[96 - 32 * j : 96 - 32 * j + WINDOW, :],
                preferred_element_type=F32,
            )
            for h in range(PER_X):
                lanes = slice(KP * (4 * h + j), KP * (4 * h + j + 1))
                packed[x, :, lanes] = full[RP * h : RP * (h + 1)].astype(BF16)
        for y in range(2):
            send(x, y).start()
    for copy in copies[3:]:
        copy.wait()
    row_energy = eps_a[0, a] - to_rows(eps_occ[...], ROWS, first)
    for b in range(SLABS):
        energy[b] = row_energy + (eps_b[0, b] - eps_occ[...])
        same[b] = jnp.where(row[:ROWS] == (b_irrep[0, b] ^ occ[...]), 1.0, 0.0)
    for x in range(XS):
        for y in range(2):
            send(x, y).wait()


def mm_kernel(t_ref, w_ref, out_ref):
    none = jnp.zeros((NP - SP, ZS * KP), BF16)
    rows = []
    for c in range(CS):
        rows += [jnp.concatenate([w_ref[CS * z + c] for z in range(ZS)], axis=1), none]
    w_t = jnp.concatenate(rows, axis=0)
    out_ref[...] = lax.dot_general(
        t_ref[...], w_t, (((1,), (1,)), ((), ())), preferred_element_type=F32
    )


def end_kernel(energy_ref, same_ref, part_ref, out_ref):
    for b in range(SLABS):
        low, c = divmod(b, CS)
        lanes = slice(NP * c, NP * c + O)
        total = part_ref[low, :ROWS, lanes]
        for x in range(1, XS):
            total = total + part_ref[2 * x + low, :ROWS, lanes]
        total = jnp.where(same_ref[b] > 0.5, total, 0.0)
        out_ref[:, O * b : O * (b + 1)] = total / energy_ref[b]


def call(kernel, out, flops, moved, room, **rest):
    return pl.pallas_call(
        kernel,
        out_shape=out,
        cost_estimate=pl.CostEstimate(flops=flops, bytes_accessed=moved, transcendentals=0),
        compiler_params=pltpu.CompilerParams(vmem_limit_bytes=room * 2**20),
        **rest,
    )


def per_device(t_slab, w_cycle, a_irrep, b_irrep, c_irrep, occ_irrep, eps_a, eps_b, eps_occ):
    vmem, smem, dma = pltpu.VMEM, pltpu.SMEM, pltpu.SemaphoreType.DMA
    struct = jax.ShapeDtypeStruct
    whole = pl.BlockSpec(memory_space=pltpu.VMEM)
    lanes = lambda vector: vector.reshape(1, -1)
    a_row, b_row, c_row, occ, eo = (lanes(v) for v in (a_irrep, b_irrep, c_irrep, occ_irrep, eps_occ))
    w_parts, t_near = call(
        head_kernel,
        [pltpu.HBM((2 * SLABS, SP, KP), BF16), vmem((ROWS, EARLY), BF16)],
        10**7, 10**6, 56,
        in_specs=[HBM] * 5,
        out_specs=[HBM, whole],
        scratch_shapes=[
            smem((1, 4), I32), smem((1, 512), I32), vmem((1, O), I32), vmem((COLS, O), BF16),
            vmem((SLABS, SP, KP), BF16), dma((4,)), dma, dma((2 * SLABS,)),
        ],
    )(b_row, c_row, occ, w_cycle.T, t_slab)
    w_got = lax.all_to_all(w_parts, "rep", split_axis=0, concat_axis=0, tiled=True)
    w_own = jnp.sum(w_got, axis=0, dtype=BF16)
    t_parts, energy, same = call(
        t_kernel,
        [pltpu.HBM((2 * XS, RP, ZS * KP), BF16), vmem((SLABS, ROWS, O), F32), vmem((SLABS, ROWS, O), F32)],
        4 * 10**9, 4 * 10**6, 55,
        in_specs=[HBM] * 7 + [whole, HBM],
        out_specs=[HBM, whole, whole],
        scratch_shapes=[
            smem((1, 128), I32), vmem((1, 512), I32), vmem((1, O), I32), smem((1, 4), I32), smem((1, 128), F32),
            smem((1, 4), F32), vmem((1, O), F32), vmem((ROWS, EARLY), BF16), vmem((RP, CHUNK), BF16), vmem((CHUNKS, CHUNK), F32),
            vmem((WINDOW + 96, KP), BF16), vmem((CHUNKS * RP, CHUNK), BF16), vmem((XS, RP, ZS * KP), BF16),
            dma((7,)), dma, dma((2 * XS,)),
        ],
    )(
        a_row, c_row, occ, b_row, lanes(eps_a), lanes(eps_b), eo,
        pltpu.with_memory_space_constraint(t_near, pltpu.VMEM), t_slab,
    )
    t_got = lax.all_to_all(
        t_parts, ("idx", "rep"), split_axis=0, concat_axis=0, axis_index_groups=WORK_GROUPS, tiled=True
    )
    w_own, t_parts = lax.optimization_barrier((w_own, t_parts))
    w_z = lax.all_gather(w_own, ("idx", "rep"), axis=0, axis_index_groups=Z_CORE_GROUPS)
    partial = call(
        mm_kernel, struct((2 * XS * RP, CS * NP), F32), 2 * 512 * 2048 * 128, 3 * 10**6, 24,
        in_specs=[whole] * 2, out_specs=whole,
    )(t_got.reshape(-1, ZS * KP), w_z)
    ends = lax.all_to_all(
        partial.reshape(2 * XS, RP, CS * NP), ("idx", "rep"), split_axis=0, concat_axis=0,
        axis_index_groups=WORK_GROUPS, tiled=True,
    )
    return call(
        end_kernel, struct((ROWS, COLS), F32), 10**6, 10**6, 24, in_specs=[whole] * 3, out_specs=whole
    )(*(pltpu.with_memory_space_constraint(near, pltpu.VMEM) for near in (energy, same)), ends)


def solution(mesh):
    in_specs = (P(("idx", "rep"), None), P(("idx", "rep"), None), P(), P(), P(), P(), P(), P(), P())
    out_specs = P(("idx", "rep"), None)
    return jax.shard_map(
        per_device, mesh=mesh, in_specs=in_specs, out_specs=out_specs, check_vma=False
    )
```

```python
import jax
import jax.numpy as jnp
from jax import lax
from jax.experimental import pallas as pl
from jax.experimental.pallas import tpu as pltpu
from jax.sharding import PartitionSpec as P

O = 100
G = 8
COLS = 400
SLABS = 4
SP = 112
NP = 128
KP = 128
RP = 32
ROWS = 25
STACK = 56
GROUP = G * O
CHUNK = 4 * GROUP
CHUNKS = 16
PER_X = 4
EARLY = CHUNKS // 2 * CHUNK
WINDOW = 896
F32, BF16, I32 = jnp.float32, jnp.bfloat16, jnp.int32
HBM = pl.BlockSpec(memory_space=pltpu.HBM)
ZS, XS, YS, CS = 16, 4, 4, 2
Z_GROUPS = [[x * ZS + z for z in range(ZS)] for x in range(XS)]
WORK_GROUPS = [
    [(x * ZS + z) * YS * CS + (2 * high + low) * CS + c for x in range(XS) for low in range(2)]
    for z in range(ZS)
    for high in range(2)
    for c in range(CS)
]
Z_CORE_GROUPS = [
    [(x * ZS + z) * YS * CS + y * CS + c for z in range(ZS) for c in range(CS)]
    for x in range(XS)
    for y in range(YS)
]


def iota(shape, dim):
    return lax.broadcasted_iota(I32, shape, dim)


def mod_o(n):
    return n - O * jnp.floor((n.astype(F32) + 0.5) * (1.0 / O)).astype(I32)


def to_rows(lanes, count, first):
    shape = (count, lanes.shape[1])
    hit = iota(shape, 1) == iota(shape, 0) + first
    return jnp.sum(jnp.where(hit, lanes, 0.0), axis=1, keepdims=True)


def lookup(lanes, index):
    parts = [
        jnp.take_along_axis(lanes, index[:, at : at + 128], axis=1) for at in range(0, index.shape[1], 128)
    ]
    return jnp.concatenate(parts, axis=1)


def fetch(sources, targets, sems):
    copies = [pltpu.make_async_copy(s, t, sems.at[i]) for i, (s, t) in enumerate(zip(sources, targets))]
    for copy in copies:
        copy.start()
    return copies


def place():
    return lax.axis_index("idx") * (YS * CS) + lax.axis_index("rep")


def padded(lanes):
    wide = jnp.concatenate([lanes, jnp.zeros((1, 128 - O), lanes.dtype)], axis=1)
    return jnp.broadcast_to(wide, (8, 128))


def head_kernel(
    b_hbm, c_hbm, occ_hbm, w_hbm, t_hbm, out_hbm, t_ref, b_irrep, c_irrep, occ, w_ref, out_ref, sems, t_sem, out_sem
):
    copies = fetch((b_hbm, c_hbm, occ_hbm, w_hbm), (b_irrep, c_irrep, occ, w_ref), sems)
    early = pltpu.make_async_copy(t_hbm.at[:, pl.ds(0, EARLY)], t_ref, t_sem)
    early.start()
    out_ref[...] = jnp.zeros_like(out_ref)
    for copy in copies[:3]:
        copy.wait()
    column = to_rows(occ[...].astype(F32), O, 0).astype(I32)
    same = column ^ (c_irrep[0, place()] ^ occ[...])
    kept = [same == b_irrep[0, b] for b in range(SLABS)]
    copies[3].wait()
    w = w_ref[...].astype(F32)
    sends = []
    for b in range(SLABS):
        out_ref[b, :O, :O] = jnp.where(kept[b], w[O * b : O * (b + 1)], 0.0).astype(BF16)
        for high in range(2):
            at = SLABS * high + b
            sends.append(pltpu.make_async_copy(out_ref.at[b], out_hbm.at[at], out_sem.at[at]))
            sends[-1].start()
    for send in sends:
        send.wait()
    early.wait()


def t_kernel(
    a_hbm, c_hbm, occ_hbm, b_hbm, ea_hbm, eb_hbm, eo_hbm, early, t_hbm, out_hbm, energy, same,
    a_irrep, c_lanes, occ, b_irrep, eps_a, eps_b, eps_occ, late, want, have, pick, kept, packed, sems, t_sem, o_sems,
):
    def send(x, y):
        return pltpu.make_async_copy(packed.at[x], out_hbm.at[2 * x + y], o_sems.at[2 * x + y])

    copies = fetch(
        (a_hbm, c_hbm, occ_hbm, b_hbm, ea_hbm, eb_hbm, eo_hbm),
        (a_irrep, c_lanes, occ, b_irrep, eps_a, eps_b, eps_occ),
        sems,
    )
    rest = pltpu.make_async_copy(t_hbm.at[:, pl.ds(EARLY, EARLY)], late, t_sem)
    rest.start()
    at = iota((WINDOW + 96, 1), 0) - 96
    k = jnp.where((at >= 0) & (at < GROUP), mod_o(jnp.maximum(at, 0)), -1)
    pick[...] = jnp.where(k == iota((WINDOW + 96, KP), 1), 1.0, 0.0).astype(BF16)
    for q in range(CHUNKS):
        kept[RP * q + 16 : RP * q + RP, :] = jnp.zeros((16, CHUNK), BF16)
    lane = iota((8, CHUNK), 1)
    mod = mod_o(lane)
    over = (lane - mod) // O
    group = iota((8, 128), 0) // 4
    for copy in copies[:3]:
        copy.wait()
    here = place()
    a, first = here // 4, ROWS * (here % 4)
    row = a_irrep[0, a] ^ to_rows(occ[...].astype(F32), RP, first).astype(I32)
    occ_t = lookup(padded(occ[...]), mod)
    want[...] = (row ^ occ_t[:1]).astype(BF16)
    for half in range(2):
        lanes = [jnp.broadcast_to(c_lanes[:, 128 * v : 128 * v + 128], (8, 128)) for v in (2 * half, 2 * half + 1)]
        source = jnp.where(group == 0, lanes[0], lanes[1])
        have[8 * half : 8 * half + 8, :] = lookup(source, 32 * (iota((8, CHUNK), 0) % 4) + over).astype(F32)
    for x in range(XS):
        if x == XS // 2:
            rest.wait()
        source, skip = (early, 0) if x < XS // 2 else (late, EARLY)
        part = slice(RP * PER_X * x, RP * PER_X * (x + 1))
        for q in range(PER_X * x, PER_X * (x + 1)):
            mask = want[:ROWS, :] == have[q : q + 1, :].astype(BF16)
            got = source[:, CHUNK * q - skip : CHUNK * (q + 1) - skip]
            kept[RP * q : RP * q + ROWS, :] = jnp.where(mask, got, jnp.zeros((), BF16))
        for j in range(4):
            full = jnp.dot(
                kept[part, 768 * j : 768 * j + WINDOW],
                pick[96 - 32 * j : 96 - 32 * j + WINDOW, :],
                preferred_element_type=F32,
            )
            for h in range(PER_X):
                lanes = slice(KP * (4 * h + j), KP * (4 * h + j + 1))
                packed[x, :, lanes] = full[RP * h : RP * (h + 1)].astype(BF16)
        for y in range(2):
            send(x, y).start()
    for copy in copies[3:]:
        copy.wait()
    row_energy = eps_a[0, a] - to_rows(eps_occ[...], ROWS, first)
    for b in range(SLABS):
        energy[b] = row_energy + (eps_b[0, b] - eps_occ[...])
        same[b] = jnp.where(row[:ROWS] == (b_irrep[0, b] ^ occ[...]), 1.0, 0.0)
    for x in range(XS):
        for y in range(2):
            send(x, y).wait()


def mm_kernel(t_ref, w_ref, out_ref):
    none = jnp.zeros((NP - SP, ZS * KP), BF16)
    rows = []
    for c in range(CS):
        rows += [jnp.concatenate([w_ref[CS * z + c] for z in range(ZS)], axis=1), none]
    w_t = jnp.concatenate(rows, axis=0)
    got = lax.dot_general(t_ref[...], w_t, (((1,), (1,)), ((), ())), preferred_element_type=F32)
    for to in range(2 * XS):
        for c in range(CS):
            out_ref[to, ROWS * c : ROWS * (c + 1), :] = got[RP * to : RP * to + ROWS, NP * c : NP * (c + 1)]
        out_ref[to, CS * ROWS :, :] = jnp.zeros((STACK - CS * ROWS, NP), F32)


def end_kernel(energy_ref, same_ref, part_ref, out_ref):
    for b in range(SLABS):
        low, c = divmod(b, CS)
        rows = slice(ROWS * c, ROWS * (c + 1))
        total = part_ref[low, rows, :O]
        for x in range(1, XS):
            total = total + part_ref[2 * x + low, rows, :O]
        total = jnp.where(same_ref[b] > 0.5, total, 0.0)
        out_ref[:, O * b : O * (b + 1)] = total / energy_ref[b]


def call(kernel, out, flops, moved, room, **rest):
    return pl.pallas_call(
        kernel,
        out_shape=out,
        cost_estimate=pl.CostEstimate(flops=flops, bytes_accessed=moved, transcendentals=0),
        compiler_params=pltpu.CompilerParams(vmem_limit_bytes=room * 2**20),
        **rest,
    )


def per_device(t_slab, w_cycle, a_irrep, b_irrep, c_irrep, occ_irrep, eps_a, eps_b, eps_occ):
    vmem, smem, dma = pltpu.VMEM, pltpu.SMEM, pltpu.SemaphoreType.DMA
    struct = jax.ShapeDtypeStruct
    whole = pl.BlockSpec(memory_space=pltpu.VMEM)
    lanes = lambda vector: vector.reshape(1, -1)
    a_row, b_row, c_row, occ, eo = (lanes(v) for v in (a_irrep, b_irrep, c_irrep, occ_irrep, eps_occ))
    w_parts, t_near = call(
        head_kernel,
        [pltpu.HBM((2 * SLABS, SP, KP), BF16), vmem((ROWS, EARLY), BF16)],
        10**7, 10**6, 56,
        in_specs=[HBM] * 5,
        out_specs=[HBM, whole],
        scratch_shapes=[
            smem((1, 4), I32), smem((1, 512), I32), vmem((1, O), I32), vmem((COLS, O), BF16),
            vmem((SLABS, SP, KP), BF16), dma((4,)), dma, dma((2 * SLABS,)),
        ],
    )(b_row, c_row, occ, w_cycle.T, t_slab)
    w_got = lax.all_to_all(w_parts, "rep", split_axis=0, concat_axis=0, tiled=True)
    w_own = jnp.sum(w_got, axis=0, dtype=BF16)
    t_parts, energy, same = call(
        t_kernel,
        [pltpu.HBM((2 * XS, RP, ZS * KP), BF16), vmem((SLABS, ROWS, O), F32), vmem((SLABS, ROWS, O), F32)],
        4 * 10**9, 4 * 10**6, 55,
        in_specs=[HBM] * 7 + [whole, HBM],
        out_specs=[HBM, whole, whole],
        scratch_shapes=[
            smem((1, 128), I32), vmem((1, 512), I32), vmem((1, O), I32), smem((1, 4), I32), smem((1, 128), F32),
            smem((1, 4), F32), vmem((1, O), F32), vmem((ROWS, EARLY), BF16), vmem((RP, CHUNK), BF16), vmem((CHUNKS, CHUNK), F32),
            vmem((WINDOW + 96, KP), BF16), vmem((CHUNKS * RP, CHUNK), BF16), vmem((XS, RP, ZS * KP), BF16),
            dma((7,)), dma, dma((2 * XS,)),
        ],
    )(
        a_row, c_row, occ, b_row, lanes(eps_a), lanes(eps_b), eo,
        pltpu.with_memory_space_constraint(t_near, pltpu.VMEM), t_slab,
    )
    t_got = lax.all_to_all(
        t_parts, ("idx", "rep"), split_axis=0, concat_axis=0, axis_index_groups=WORK_GROUPS, tiled=True
    )
    w_own, t_parts = lax.optimization_barrier((w_own, t_parts))
    w_z = lax.all_gather(w_own, ("idx", "rep"), axis=0, axis_index_groups=Z_CORE_GROUPS)
    partial = call(
        mm_kernel, struct((2 * XS, STACK, NP), F32), 2 * 512 * 2048 * 128, 3 * 10**6, 24,
        in_specs=[whole] * 2, out_specs=whole,
    )(t_got.reshape(-1, ZS * KP), w_z)
    ends = lax.all_to_all(
        partial, ("idx", "rep"), split_axis=0, concat_axis=0,
        axis_index_groups=WORK_GROUPS, tiled=True,
    )
    return call(
        end_kernel, struct((ROWS, COLS), F32), 10**6, 10**6, 24, in_specs=[whole] * 3, out_specs=whole
    )(*(pltpu.with_memory_space_constraint(near, pltpu.VMEM) for near in (energy, same)), ends)


def solution(mesh):
    in_specs = (P(("idx", "rep"), None), P(("idx", "rep"), None), P(), P(), P(), P(), P(), P(), P())
    out_specs = P(("idx", "rep"), None)
    return jax.shard_map(
        per_device, mesh=mesh, in_specs=in_specs, out_specs=out_specs, check_vma=False
    )
```
